256 devices in a mesh: row: 32 (over y, z_hi, core), col: 8 (over z_lo, x).
Axes of the slice: x: 4, y: 4, z: 8 (z_hi: 4, z_lo: 2; z = z_hi * 2 + z_lo), core: 2. Of those that a mesh axis runs over, the one named last changes fastest.
Arguments:
- src_pos: float32 [128, 65536], P('col', 'row'), may hold values from -1 to 1
- tgt_pos: float32 [128, 16384], P('row', 'col'), may hold values from -1 to 1
- coupling: bfloat16 [65536, 16384], P('row', 'col'), may hold values from 0 to 36, as said below
- prior_tgt: float32 [16384], P('col'), may hold values from -4 to 4
Outputs:
- src_potential: float32 [65536], P('row')
- tgt_potential: float32 [16384], P('col')
The draws below stay inside these ranges and needn't reach their ends.
Inputs may be any that keep to these rules, and one draw needn't show every extreme that they name: `coupling`: all entries are positive.
All inputs are finite; a program needn't handle non-finite values.
Results may differ from the reference program's by a relative error of at most 0.0003.
Values sent between devices are 32-bit elements; how exact they have to be, the bound alone decides.
A program may use at most 128 MiB of HBM per device.

```python
import math
import jax
import jax.numpy as jnp
from jax import lax

D = 128
RANK = 130
N_DEV = 2048
SWEEPS = 2
N = 65536
M = 16384
N_ROW = 32


cluster_count = 8


center_weight = 0.95


noise_weight = 0.31


matched_boost = 14.0


coupling_norm = 14.0


def cluster_layout(key):
    labels_src = jax.random.randint(jax.random.fold_in(key, 201), (N,), 0, cluster_count)
    labels_tgt = jax.random.randint(jax.random.fold_in(key, 202), (M,), 0, cluster_count)
    centers = jnp.clip(jax.random.normal(jax.random.fold_in(key, 203), (D, cluster_count), jnp.float32), -4.0, 4.0)
    return (labels_src, labels_tgt, centers)


def embed(centers, labels, noise, scale):
    mixed = center_weight * jnp.take(centers, labels, axis=1) + noise_weight * noise
    return jnp.clip(mixed * scale / math.sqrt(D), -1.0, 1.0).astype(jnp.float32)


def draw_src_pos(key, part):
    labels_src, labels_tgt, centers = cluster_layout(key)
    key = jax.random.fold_in(key, 11)
    key_noise, key_scale = jax.random.split(key, 2)
    noise = jnp.clip(jax.random.normal(key_noise, (D, N), jnp.float32), -4.0, 4.0)
    scale = jnp.exp(jax.random.uniform(key_scale, (1, N), jnp.float32, math.log(0.7), math.log(1.4)))
    return embed(centers, labels_src, noise, scale)


def draw_tgt_pos(key, part):
    labels_src, labels_tgt, centers = cluster_layout(key)
    key = jax.random.fold_in(key, 23)
    key_noise, key_scale = jax.random.split(key, 2)
    noise = jnp.clip(jax.random.normal(key_noise, (D, M), jnp.float32), -4.0, 4.0)
    scale = jnp.exp(jax.random.uniform(key_scale, (1, M), jnp.float32, math.log(0.7), math.log(1.4)))
    return embed(centers, labels_tgt, noise, scale)


def draw_coupling(key, part):
    labels_src, labels_tgt, centers = cluster_layout(key)
    key = jax.random.fold_in(key, 37)
    base = jnp.exp(jax.random.uniform(key, (N, M), jnp.float32, math.log(0.25), math.log(4.0)))
    matched = labels_src[:, None] == labels_tgt[None, :]
    boost = jnp.where(matched, matched_boost, 1.0)
    row_rise = 1.0 + 2.0 * jnp.arange(N, dtype=jnp.float32) / N
    col_rise = 1.0 + 2.0 * jnp.arange(M, dtype=jnp.float32) / M
    return (base * boost * row_rise[:, None] * col_rise[None, :] / coupling_norm).astype(jnp.bfloat16)


def levels(stream_key, shape, cuts, smallest, high):
    def one(axis_at, shards_of):
        draws = jax.random.uniform(jax.random.fold_in(jax.random.fold_in(stream_key, 6), axis_at), (shards_of,), jnp.float32, smallest / len(cuts), high / len(cuts))
        return jnp.repeat(jnp.exp(draws), shape[axis_at] // shards_of).reshape((-1,) + (1,) * (len(shape) - axis_at - 1))

    level = one(*cuts[0])
    for cut in cuts[1:]:
        level = level * one(*cut)
    return level


def scatter_about(own_key, extent, scale, most, shards=(), kind=jnp.bfloat16):
    factor_of = levels(own_key, extent, shards, -0.22, 0.18) if shards else 1.0
    values = jax.random.normal(own_key, extent, jnp.float32) * scale * factor_of
    return jnp.minimum(jnp.maximum(values, -most), most).astype(kind)


def setup_inputs(seed: int = 0) -> dict:
    key_list = jax.random.split(jax.random.key(seed), 5)
    return {
        "src_pos": draw_src_pos(jax.random.fold_in(key_list[4], 71), 0),
        "tgt_pos": draw_tgt_pos(jax.random.fold_in(key_list[4], 71), 0),
        "coupling": draw_coupling(jax.random.fold_in(key_list[4], 71), 0),
        "prior_tgt": scatter_about(key_list[3], (M,), 1.0, 4.0, ((0, 8),), jnp.float32),
    }


EPSILON = 0.25


def factors(positions):
    squared = jnp.sum(positions * positions, axis=0, keepdims=True)
    unit_row = jnp.ones_like(squared)
    left_side = jnp.concatenate([positions, squared, unit_row], axis=0)
    right_side = jnp.concatenate([-2.0 * positions, unit_row, squared], axis=0)
    return left_side, right_side.astype(jnp.bfloat16)


def reference(src_pos, tgt_pos, coupling, prior_tgt):
    src_left, src_right = factors(src_pos)
    tgt_left, tgt_right = factors(tgt_pos)
    blocks = coupling.reshape(N_ROW, N_DEV, M)
    right_blocks = src_right.reshape(RANK, N_ROW, N_DEV).transpose(1, 0, 2)

    def add_block(summed, pieces):
        piece_right, piece = pieces
        return summed + jnp.dot(piece_right, piece, preferred_element_type=jnp.float32), None

    panel_sum, _ = lax.scan(add_block, jnp.zeros((RANK, M), jnp.float32), (right_blocks, blocks))
    core_matrix = lax.dot_general(panel_sum, tgt_right.astype(jnp.float32), (((1,), (1,)), ((), ())),
                                  precision=lax.Precision.HIGHEST)
    core_matrix = core_matrix / (N * M)
    left_blocks = src_left.reshape(RANK, N_ROW, N_DEV).transpose(1, 0, 2)

    def cost_block(left_piece):
        rows_core = lax.dot_general(left_piece, core_matrix, (((0,), (0,)), ((), ())),
                                    precision=lax.Precision.HIGHEST)
        return -2.0 * jnp.dot(rows_core, tgt_left, precision=lax.Precision.HIGHEST)

    shift_src = -EPSILON * math.log(N)
    shift_tgt = -EPSILON * math.log(M)

    def row_update(target_pot):
        def one_block(left_piece):
            values = (target_pot[None, :] - cost_block(left_piece)) / EPSILON
            return shift_src - EPSILON * jax.nn.logsumexp(values, axis=1)
        return lax.map(one_block, left_blocks).reshape(N)

    def col_update(source_pot):
        source_blocks = source_pot.reshape(N_ROW, N_DEV)

        def step_block(carry, pieces):
            highest, summed = carry
            left_piece, source_piece = pieces
            values = (source_piece[:, None] - cost_block(left_piece)) / EPSILON
            top_now = jnp.maximum(highest, jnp.max(values, axis=0))
            summed = summed * jnp.exp(highest - top_now) + jnp.sum(jnp.exp(values - top_now[None, :]), axis=0)
            return (top_now, summed), None

        start = (jnp.full((M,), -jnp.inf, jnp.float32), jnp.zeros((M,), jnp.float32))
        (highest, summed), _ = lax.scan(step_block, start, (left_blocks, source_blocks))
        return shift_tgt - EPSILON * (highest + jnp.log(summed))

    target_pot = prior_tgt
    source_pot = jnp.zeros((N,), jnp.float32)
    for repeat in range(SWEEPS):
        source_pot = row_update(target_pot)
        target_pot = col_update(source_pot)
    return source_pot, target_pot
```

```python
import math

import jax
import jax.numpy as jnp
from jax import lax
from jax.experimental import pallas as pl
from jax.experimental.pallas import tpu as pltpu
from jax.sharding import PartitionSpec as P

SWEEPS = 2
EPSILON = 0.25
LOG2E = 1.4426950408889634
MESH = pl.DeviceIdType.MESH
F32 = jnp.float32
BF16 = jnp.bfloat16
LOW = -3.0e38

SRC, TGT_Z, TGT_Y, TGT_C, SCATTER, MIDDLE, SPREAD, ROWS, PAIR, CHIPS, LOCAL_W, LOCAL_S, LOCAL_T = (
    0, 1, 2, 3, 4, 5, 6, 7, 9, 11, 13, 14, 15,
)


def split(value):
    high = value.astype(BF16)
    return high, (value - high.astype(F32)).astype(BF16)


def feature_major(x_ref, stack):
    size = x_ref.shape[1]

    def block(b, carry):
        cols = pl.ds(pl.multiple_of(b * 512, 512), 512)
        x = x_ref[:, cols]
        high, low = split(x)
        stack[0:128, cols] = high
        stack[128:256, cols] = low
        stack[256:384, cols] = high
        q = jnp.sum(x * x, axis=0, keepdims=True)
        q_high = q.astype(BF16).astype(F32)
        q_low = q - q_high
        at = lax.broadcasted_iota(jnp.int32, (16, 512), 0)
        ext = jnp.where((at == 1) | (at == 5), 1.0, 0.0)
        ext = jnp.where((at == 0) | (at == 4), q_high, ext)
        ext = jnp.where(at == 2, q_low, ext)
        stack[384:400, cols] = ext.astype(BF16)
        stack[400:512, cols] = jnp.zeros((112, 512), BF16)
        return carry

    lax.fori_loop(0, size // 512, block, 0)


def state_major(x_ref, stack):
    size = x_ref.shape[1]

    def block(b, carry):
        at = pl.ds(pl.multiple_of(b * 128, 128), 128)
        x = x_ref[:, at].T
        high, low = split(x)
        stack[at, 0:128] = high
        stack[at, 128:256] = low
        stack[at, 256:384] = high
        q = jnp.sum(x * x, axis=1, keepdims=True)
        q_high = q.astype(BF16).astype(F32)
        q_low = q - q_high
        lane = lax.broadcasted_iota(jnp.int32, (128, 128), 1)
        ext = jnp.where((lane == 1) | (lane == 5), 1.0, 0.0)
        ext = jnp.where((lane == 0) | (lane == 4), q_high, ext)
        ext = jnp.where(lane == 2, q_low, ext)
        stack[at, 384:512] = ext.astype(BF16)
        return carry

    lax.fori_loop(0, size // 128, block, 0)


def down_rows(vector, out):
    for b in range(vector.shape[0]):
        out[128 * b : 128 * (b + 1), :] = jnp.broadcast_to(vector[b : b + 1, :], (128, 128)).T


CHUNK = 64
STRIP = 256


def reduce_strip(n, pot, cost, out):
    lanes = pl.ds(pl.multiple_of(n * STRIP, STRIP), STRIP)

    def chunk(k, carry):
        top, summed = carry
        rows = pl.ds(pl.multiple_of(k * CHUNK, CHUNK), CHUNK)
        p = pot[rows, :]
        values = jnp.concatenate([p] * (STRIP // 128), axis=1) - cost[rows, lanes]
        values = values.reshape(CHUNK // 8, 8, STRIP)
        now = jnp.maximum(top, jnp.max(values, axis=0))
        summed = summed * jnp.exp2(top - now) + jnp.sum(jnp.exp2(values - now[None]), axis=0)
        return now, summed

    start = (jnp.full((8, STRIP), LOW, F32), jnp.zeros((8, STRIP), F32))
    top, summed = lax.fori_loop(0, cost.shape[0] // CHUNK, chunk, start, unroll=4)
    highest = jnp.max(top, axis=0, keepdims=True)
    total = jnp.sum(summed * jnp.exp2(top - highest), axis=0, keepdims=True)
    result = highest + LOG2E * jnp.log(total)
    for t in range(STRIP // 128):
        out[pl.ds(n * (STRIP // 128) + t, 1), :] = result[:, 128 * t : 128 * (t + 1)]


def combine(buffer):
    n = buffer.shape[0]
    top = buffer[0]
    for k in range(1, n):
        top = jnp.maximum(top, buffer[k])
    total = jnp.exp2(buffer[0] - top)
    for k in range(1, n):
        total = total + jnp.exp2(buffer[k] - top)
    return top + LOG2E * jnp.log(total)


def kernel(
    n_row, n_col, src_ref, tgt_ref, coupling_ref, prior_ref, f_ref, g_ref,
    weights, src_full, tgt_blocks, tgt_full, xs, xt, ys, yt, us, ut, panel,
    parts, gathered, middle, core, cost, cost_t, pot, local, by_col, by_pair, by_chip,
    send, recv,
):
    row, col = lax.axis_index("row"), lax.axis_index("col")
    core_id = lax.rem(row, 2)
    chip = row // 2
    n_chip = n_row // 2
    depth = lax.rem(chip, 4)
    y = chip // 4
    n_y = n_chip // 4
    sib = row + 1 - 2 * core_id
    rows_here, cols_here = coupling_ref.shape
    total_src, total_tgt = rows_here * n_row, cols_here * n_col
    group = 2 * n_col
    slot = core_id * n_col + col

    col_peers = [(row, lax.rem(col + d, n_col)) for d in range(1, n_col)]
    z_peers = [((y * 4 + lax.rem(depth + d, 4)) * 2 + core_id, col) for d in range(1, 4)]
    y_peers = [((lax.rem(y + d, n_y) * 4 + depth) * 2 + core_id, col) for d in range(1, n_y)]
    chip_peers = [(lax.rem(chip + d, n_chip) * 2 + core_id, col) for d in range(1, n_chip)]
    pair_peer = (sib, col)
    group_peers = col_peers + [(sib, lax.rem(col + d, n_col)) for d in range(n_col)]

    def put(source, target, index, peer):
        pltpu.make_async_remote_copy(
            src_ref=source, dst_ref=target, send_sem=send.at[index], recv_sem=recv.at[index],
            device_id=peer, device_id_type=MESH,
        ).start()

    def await_recv(ref, index):
        pltpu.make_async_copy(ref, ref, recv.at[index]).wait()

    def await_send(ref, index):
        pltpu.make_async_copy(ref, ref, send.at[index]).wait()

    barrier = pltpu.get_barrier_semaphore()
    greeted = group_peers + chip_peers
    for peer in greeted:
        pl.semaphore_signal(barrier, inc=1, device_id=peer, device_id_type=MESH)
    features = src_ref.shape[0]
    mine = pl.ds(pl.multiple_of(col * features, features), features)
    copy_w = pltpu.make_async_copy(coupling_ref, weights, recv.at[LOCAL_W])
    copy_s = pltpu.make_async_copy(src_ref, src_full.at[mine], recv.at[LOCAL_S])
    copy_t = pltpu.make_async_copy(tgt_ref, tgt_blocks.at[core_id, chip], recv.at[LOCAL_T])
    copy_t.start()
    copy_s.start()
    copy_w.start()
    pl.semaphore_wait(barrier, len(greeted))

    for peer in z_peers:
        put(tgt_ref, tgt_blocks.at[core_id, chip], TGT_Z, peer)
    for peer in col_peers:
        put(src_ref, src_full.at[mine], SRC, peer)
    copy_t.wait()
    await_recv(tgt_blocks.at[0, 0:3], TGT_Z)
    plane = pl.ds(y * 4, 4)
    for peer in y_peers:
        put(tgt_blocks.at[core_id, plane], tgt_blocks.at[core_id, plane], TGT_Y, peer)

    copy_s.wait()
    await_recv(src_full.at[0 : features * (n_col - 1)], SRC)
    await_recv(tgt_blocks.at[0, 0 : 4 * (n_y - 1)], TGT_Y)
    put(tgt_blocks.at[core_id], tgt_blocks.at[core_id], TGT_C, pair_peer)
    feature_major(src_full, xs)
    copy_w.wait()

    def panel_strip(n, carry):
        cols = pl.ds(pl.multiple_of(n * 256, 256), 256)
        panel[:, cols] = jnp.dot(xs[256:400, :], weights[:, cols], preferred_element_type=F32)
        return carry

    lax.fori_loop(0, cols_here // 256, panel_strip, 0)

    await_recv(tgt_blocks.at[0], TGT_C)
    for k in range(n_chip):
        tgt_full[8 * k : 8 * k + 8, :] = jnp.concatenate([tgt_blocks[0, k], tgt_blocks[1, k]], axis=0)
    feature_major(tgt_full, ys)

    part = jnp.zeros((144, 256), F32)
    whole = panel[...]
    for _ in range(3):
        term = whole.astype(BF16)
        whole = whole - term.astype(F32)
        part = part + lax.dot_general(
            term, ys[256:512, :], (((1,), (1,)), ((), ())), preferred_element_type=F32
        )
    at8 = lax.broadcasted_iota(jnp.int32, (8, 128), 0)
    lane8 = lax.broadcasted_iota(jnp.int32, (8, 128), 1)
    edge = jnp.where(at8 < 2, part[128:136, 0:128], 0.0)
    corner = part[128:136, 128:256]
    corner = jnp.concatenate([corner[6:8], corner[0:6]], axis=0)
    edge = jnp.where((at8 >= 2) & (at8 < 4), corner, edge)
    side = jnp.where(at8 < 2, part[0:128, 128:256].T[0:8], 0.0)
    for s in range(group):
        parts[s, 0:8, :] = part[8 * s : 8 * s + 8, 0:128]
        one = edge[s : s + 1] if s < 8 else side[s - 8 : s - 7]
        parts[s, 8:16, :] = jnp.where(at8 == 0, one, 0.0)

    def slot_of(peer):
        return lax.rem(peer[0], 2) * n_col + peer[1]

    for peer in group_peers:
        put(parts.at[slot_of(peer)], gathered.at[slot], SCATTER, peer)
    gathered[slot] = parts[slot]
    state_major(src_full, xt)
    await_recv(gathered.at[0 : group - 1], SCATTER)
    total = gathered[0]
    for k in range(1, group):
        total = total + gathered[k]
    middle[chip] = total
    for peer in chip_peers:
        put(middle.at[chip], middle.at[chip], MIDDLE, peer)
    state_major(tgt_full, yt)
    down_rows(prior_ref[...] * (LOG2E / EPSILON), pot)
    await_recv(middle.at[0 : n_chip - 1], MIDDLE)
    total = middle[0]
    for k in range(1, n_chip):
        total = total + middle[k]
    core[slot] = total
    for peer in group_peers:
        put(core.at[slot], core.at[slot], SPREAD, peer)
    await_recv(core.at[0 : group - 1], SPREAD)

    scale = -2.0 * LOG2E / (EPSILON * total_src * total_tgt)
    main = jnp.concatenate([core[s, 0:8, :] for s in range(group)], axis=0) * (4.0 * scale)
    src_q, src_one = core[0, 8:9, :], core[1, 8:9, :]
    corner_q, corner_one = core[2, 8:9, :], core[3, 8:9, :]
    tgt_q, tgt_one = core[8, 8:9, :], core[9, 8:9, :]

    def pattern(at, first, second):
        value = jnp.where((at == 0) | (at == 2) | (at == 4), first, 0.0)
        return jnp.where((at == 1) | (at == 5), second, value)

    at16 = lax.broadcasted_iota(jnp.int32, (128, 128), 0)
    lane16 = lax.broadcasted_iota(jnp.int32, (128, 128), 1)
    lower_left = pattern(at16, src_one, src_q) * (-2.0 * scale)
    upper_right = pattern(at16, tgt_one, tgt_q).T * (-2.0 * scale)
    lower_right = pattern(
        at16,
        pattern(lane16, corner_one[:, 1:2], corner_one[:, 0:1]),
        pattern(lane16, corner_q[:, 1:2], corner_q[:, 0:1]),
    ) * scale
    left = jnp.concatenate([main, lower_left], axis=0)
    right = jnp.concatenate([upper_right, lower_right], axis=0)
    left_high, left_low = split(left)
    right_high, right_low = split(right)
    right_lane = lax.broadcasted_iota(jnp.int32, (256, 128), 1)
    ext = jnp.where(right_lane < 4, right_high.astype(F32), right_low.astype(F32)).astype(BF16)
    factor = jnp.concatenate([left_high, left_high, left_low, ext], axis=1)

    def factor_t(b, carry):
        at = pl.ds(pl.multiple_of(b * 256, 256), 256)
        u = lax.dot_general(yt[at, :], factor, (((1,), (1,)), ((), ())), preferred_element_type=F32)
        high, low = split(u[:, 0:128])
        ut[at, 0:128] = high
        ut[at, 128:256] = high
        ut[at, 256:384] = low
        high, low = split(u[:, 128:256])
        lane = lax.broadcasted_iota(jnp.int32, (256, 128), 1)
        ut[at, 384:512] = jnp.where(lane < 4, high.astype(F32), low.astype(F32)).astype(BF16)
        return carry

    lax.fori_loop(0, cols_here // 256, factor_t, 0)

    def row_strip(n, carry):
        lanes = pl.ds(pl.multiple_of(n * STRIP, STRIP), STRIP)
        cost_t[:, lanes] = jnp.dot(ut[...], xs[:, lanes], preferred_element_type=F32)
        reduce_strip(n, pot, cost_t, local)
        return carry

    lax.fori_loop(0, rows_here // STRIP, row_strip, 0)

    def make_cost():
        def factor_n(b, carry):
            cols = pl.ds(pl.multiple_of(b * 256, 256), 256)
            u = jnp.dot(factor, ys[:, cols], preferred_element_type=F32)
            high, low = split(u[0:128])
            us[0:128, cols] = high
            us[128:256, cols] = high
            us[256:384, cols] = low
            high, low = split(u[128:256])
            at = lax.broadcasted_iota(jnp.int32, (128, 256), 0)
            us[384:512, cols] = jnp.where(at < 4, high.astype(F32), low.astype(F32)).astype(BF16)
            lanes = cols
            cost[:, lanes] = jnp.dot(xt[...], us[:, lanes], preferred_element_type=F32)
            return carry

        lax.fori_loop(0, cols_here // 256, factor_n, 0)

    def strip_pass(cost_ref):
        def body(n, carry):
            reduce_strip(n, pot, cost_ref, local)
            return carry

        lax.fori_loop(0, cost_ref.shape[1] // STRIP, body, 0)

    for sweep in range(SWEEPS):
        if sweep:
            strip_pass(cost_t)
        by_col[sweep, col] = local[...]
        for peer in col_peers:
            put(by_col.at[sweep, col], by_col.at[sweep, col], ROWS + sweep, peer)
        if sweep == 0:
            make_cost()
        await_recv(by_col.at[sweep, 0 : n_col - 1], ROWS + sweep)
        f = -math.log2(total_src) - combine(by_col.at[sweep])
        down_rows(f, pot)
        strip_pass(cost)
        by_pair[sweep, core_id] = local[...]
        put(by_pair.at[sweep, core_id], by_pair.at[sweep, core_id], PAIR + sweep, pair_peer)
        await_recv(by_pair.at[sweep, 0], PAIR + sweep)
        by_chip[sweep, chip] = combine(by_pair.at[sweep])
        for peer in chip_peers:
            put(by_chip.at[sweep, chip], by_chip.at[sweep, chip], CHIPS + sweep, peer)
        await_recv(by_chip.at[sweep, 0 : n_chip - 1], CHIPS + sweep)
        g = -math.log2(total_tgt) - combine(by_chip.at[sweep])
        if sweep + 1 < SWEEPS:
            down_rows(g, pot)
    f_ref[...] = f * (EPSILON / LOG2E)
    g_ref[...] = g * (EPSILON / LOG2E)

    await_send(src_full.at[0 : features * (n_col - 1)], SRC)
    await_send(tgt_blocks.at[0, 0:3], TGT_Z)
    await_send(tgt_blocks.at[0, 0 : 4 * (n_y - 1)], TGT_Y)
    await_send(tgt_blocks.at[0], TGT_C)
    await_send(gathered.at[0 : group - 1], SCATTER)
    await_send(middle.at[0 : n_chip - 1], MIDDLE)
    await_send(core.at[0 : group - 1], SPREAD)
    for sweep in range(SWEEPS):
        await_send(by_col.at[sweep, 0 : n_col - 1], ROWS + sweep)
        await_send(by_pair.at[sweep, 0], PAIR + sweep)
        await_send(by_chip.at[sweep, 0 : n_chip - 1], CHIPS + sweep)


def solution(mesh):
    n_row, n_col = mesh.shape["row"], mesh.shape["col"]
    n_chip = n_row // 2
    group = 2 * n_col

    def local(src_pos, tgt_pos, coupling, prior_tgt):
        rows, cols = coupling.shape
        vmem = pl.BlockSpec(memory_space=pltpu.VMEM)
        anywhere = pl.BlockSpec(memory_space=pl.ANY)
        f, g = pl.pallas_call(
            lambda *refs: kernel(n_row, n_col, *refs),
            out_shape=[
                jax.ShapeDtypeStruct((rows // 128, 128), F32),
                jax.ShapeDtypeStruct((cols // 128, 128), F32),
            ],
            in_specs=[anywhere, anywhere, anywhere, vmem],
            out_specs=[vmem, vmem],
            scratch_shapes=[
                pltpu.VMEM((rows, cols), BF16),
                pltpu.VMEM((128, rows), F32),
                pltpu.VMEM((2, n_chip, 4, cols), F32),
                pltpu.VMEM((128, cols), F32),
                pltpu.VMEM((512, rows), BF16),
                pltpu.VMEM((rows, 512), BF16),
                pltpu.VMEM((512, cols), BF16),
                pltpu.VMEM((cols, 512), BF16),
                pltpu.VMEM((512, cols), BF16),
                pltpu.VMEM((cols, 512), BF16),
                pltpu.VMEM((144, cols), F32),
                pltpu.VMEM((group, 16, 128), F32),
                pltpu.VMEM((group, 16, 128), F32),
                pltpu.VMEM((n_chip, 16, 128), F32),
                pltpu.VMEM((group, 16, 128), F32),
                pltpu.VMEM((rows, cols), F32),
                pltpu.VMEM((cols, rows), F32),
                pltpu.VMEM((max(rows, cols), 128), F32),
                pltpu.VMEM((max(rows, cols) // 128, 128), F32),
                pltpu.VMEM((SWEEPS, n_col, rows // 128, 128), F32),
                pltpu.VMEM((SWEEPS, 2, cols // 128, 128), F32),
                pltpu.VMEM((SWEEPS, n_chip, cols // 128, 128), F32),
                pltpu.SemaphoreType.DMA((16,)),
                pltpu.SemaphoreType.DMA((16,)),
            ],
            compiler_params=pltpu.CompilerParams(
                collective_id=0, has_side_effects=True, vmem_limit_bytes=63 * 2**20
            ),
        )(src_pos, tgt_pos, coupling, prior_tgt.reshape(cols // 128, 128))
        return f.reshape(rows), g.reshape(cols)

    placed = (P("col", "row"), P("row", "col"), P("row", "col"), P("col"))
    return jax.shard_map(
        local, mesh=mesh, in_specs=placed, out_specs=(P("row"), P("col")), check_vma=False
    )
```

```python
import math

import jax
import jax.numpy as jnp
from jax import lax
from jax.experimental import pallas as pl
from jax.experimental.pallas import tpu as pltpu
from jax.sharding import PartitionSpec as P

SWEEPS = 2
EPSILON = 0.25
LOG2E = 1.4426950408889634
MESH = pl.DeviceIdType.MESH
F32 = jnp.float32
BF16 = jnp.bfloat16
LOW = -3.0e38

SRC, TGT_Z, TGT_Y, TGT_C, SCATTER, MIDDLE, SPREAD, ROWS, PAIR, CHIPS, LOCAL_W, LOCAL_S, LOCAL_T = (
    0, 1, 2, 3, 4, 5, 6, 7, 9, 11, 13, 14, 15,
)
SRC_Z, TGT_Z2, TGT_Y2 = 16, 17, 18


def split(value):
    high = value.astype(BF16)
    return high, (value - high.astype(F32)).astype(BF16)


def feature_major(x_ref, stack):
    size = x_ref.shape[1]

    def block(b, carry):
        cols = pl.ds(pl.multiple_of(b * 512, 512), 512)
        x = x_ref[:, cols]
        high, low = split(x)
        stack[0:128, cols] = high
        stack[128:256, cols] = low
        stack[256:384, cols] = high
        q = jnp.sum(x * x, axis=0, keepdims=True)
        q_high = q.astype(BF16).astype(F32)
        q_low = q - q_high
        at = lax.broadcasted_iota(jnp.int32, (16, 512), 0)
        ext = jnp.where((at == 1) | (at == 5), 1.0, 0.0)
        ext = jnp.where((at == 0) | (at == 4), q_high, ext)
        ext = jnp.where(at == 2, q_low, ext)
        stack[384:400, cols] = ext.astype(BF16)
        stack[400:512, cols] = jnp.zeros((112, 512), BF16)
        return carry

    lax.fori_loop(0, size // 512, block, 0)


def state_major(x_ref, stack):
    size = x_ref.shape[1]

    def block(b, carry):
        at = pl.ds(pl.multiple_of(b * 128, 128), 128)
        x = x_ref[:, at].T
        high, low = split(x)
        stack[at, 0:128] = high
        stack[at, 128:256] = low
        stack[at, 256:384] = high
        q = jnp.sum(x * x, axis=1, keepdims=True)
        q_high = q.astype(BF16).astype(F32)
        q_low = q - q_high
        lane = lax.broadcasted_iota(jnp.int32, (128, 128), 1)
        ext = jnp.where((lane == 1) | (lane == 5), 1.0, 0.0)
        ext = jnp.where((lane == 0) | (lane == 4), q_high, ext)
        ext = jnp.where(lane == 2, q_low, ext)
        stack[at, 384:512] = ext.astype(BF16)
        return carry

    lax.fori_loop(0, size // 128, block, 0)


def down_rows(vector, out):
    for b in range(vector.shape[0]):
        out[128 * b : 128 * (b + 1), :] = jnp.broadcast_to(vector[b : b + 1, :], (128, 128)).T


CHUNK = 64
STRIP = 256


def reduce_strip(n, pot, cost, out):
    lanes = pl.ds(pl.multiple_of(n * STRIP, STRIP), STRIP)

    def chunk(k, carry):
        top, summed = carry
        rows = pl.ds(pl.multiple_of(k * CHUNK, CHUNK), CHUNK)
        p = pot[rows, :]
        values = jnp.concatenate([p] * (STRIP // 128), axis=1) - cost[rows, lanes]
        values = values.reshape(CHUNK // 8, 8, STRIP)
        now = jnp.maximum(top, jnp.max(values, axis=0))
        summed = summed * jnp.exp2(top - now) + jnp.sum(jnp.exp2(values - now[None]), axis=0)
        return now, summed

    start = (jnp.full((8, STRIP), LOW, F32), jnp.zeros((8, STRIP), F32))
    top, summed = lax.fori_loop(0, cost.shape[0] // CHUNK, chunk, start, unroll=4)
    highest = jnp.max(top, axis=0, keepdims=True)
    total = jnp.sum(summed * jnp.exp2(top - highest), axis=0, keepdims=True)
    result = highest + LOG2E * jnp.log(total)
    for t in range(STRIP // 128):
        out[pl.ds(n * (STRIP // 128) + t, 1), :] = result[:, 128 * t : 128 * (t + 1)]


def combine(buffer):
    n = buffer.shape[0]
    top = buffer[0]
    for k in range(1, n):
        top = jnp.maximum(top, buffer[k])
    total = jnp.exp2(buffer[0] - top)
    for k in range(1, n):
        total = total + jnp.exp2(buffer[k] - top)
    return top + LOG2E * jnp.log(total)


def kernel(
    n_row, n_col, src_ref, tgt_ref, coupling_ref, prior_ref, f_ref, g_ref,
    weights, src_full, tgt_blocks, tgt_full, xs, xt, ys, yt, us, ut, panel,
    parts, gathered, middle, core, cost, cost_t, pot, local, by_col, by_pair, by_chip,
    send, recv,
):
    row, col = lax.axis_index("row"), lax.axis_index("col")
    core_id = lax.rem(row, 2)
    chip = row // 2
    n_chip = n_row // 2
    depth = lax.rem(chip, 4)
    y = chip // 4
    n_y = n_chip // 4
    sib = row + 1 - 2 * core_id
    rows_here, cols_here = coupling_ref.shape
    total_src, total_tgt = rows_here * n_row, cols_here * n_col
    group = 2 * n_col
    slot = core_id * n_col + col

    x_size = n_col // 2
    x_at, plane_half = lax.rem(col, x_size), col // x_size
    half_col = (1 - plane_half) * x_size + x_at
    x_peers = [(row, plane_half * x_size + lax.rem(x_at + d, x_size)) for d in range(1, x_size)]
    half_peer = (row, half_col)
    z_near = [((y * 4 + lax.rem(depth + d, 4)) * 2 + core_id, col) for d in (1, 3)]
    z_far = ((y * 4 + lax.rem(depth + 2, 4)) * 2 + core_id, col)
    y_peers = [((lax.rem(y + d, n_y) * 4 + depth) * 2 + core_id, col) for d in range(1, n_y)]
    col_peers = [(row, lax.rem(col + d, n_col)) for d in range(1, n_col)]
    chip_peers = [(lax.rem(chip + d, n_chip) * 2 + core_id, col) for d in range(1, n_chip)]
    pair_peer = (sib, col)
    group_peers = col_peers + [(sib, lax.rem(col + d, n_col)) for d in range(n_col)]

    def put(source, target, index, peer):
        pltpu.make_async_remote_copy(
            src_ref=source, dst_ref=target, send_sem=send.at[index], recv_sem=recv.at[index],
            device_id=peer, device_id_type=MESH,
        ).start()

    def await_recv(ref, index):
        pltpu.make_async_copy(ref, ref, recv.at[index]).wait()

    def await_send(ref, index):
        pltpu.make_async_copy(ref, ref, send.at[index]).wait()

    barrier = pltpu.get_barrier_semaphore()
    greeted = x_peers + y_peers + z_near + [half_peer, pair_peer]
    for peer in greeted:
        pl.semaphore_signal(barrier, inc=1, device_id=peer, device_id_type=MESH)
    features = src_ref.shape[0]
    mine = pl.ds(pl.multiple_of(col * features, features), features)
    halfs = pl.ds(pl.multiple_of(half_col * features, features), features)
    copy_w = pltpu.make_async_copy(coupling_ref, weights, recv.at[LOCAL_W])
    copy_s = pltpu.make_async_copy(src_ref, src_full.at[mine], recv.at[LOCAL_S])
    copy_t = pltpu.make_async_copy(tgt_ref, tgt_blocks.at[core_id, chip], recv.at[LOCAL_T])
    copy_t.start()
    copy_s.start()
    copy_w.start()
    pl.semaphore_wait(barrier, len(greeted))

    for peer in z_near:
        put(tgt_ref, tgt_blocks.at[core_id, chip], TGT_Z, peer)
    put(src_ref, src_full.at[mine], SRC_Z, half_peer)
    for peer in x_peers:
        put(src_ref, src_full.at[mine], SRC, peer)
    copy_t.wait()
    await_recv(tgt_blocks.at[0, 0:2], TGT_Z)
    put(tgt_ref, tgt_blocks.at[core_id, chip], TGT_Z2, z_far)
    for d in (0, 1, 3):
        at = y * 4 + lax.rem(depth + d, 4)
        for peer in y_peers:
            put(tgt_blocks.at[core_id, at], tgt_blocks.at[core_id, at], TGT_Y, peer)
    await_recv(src_full.at[0:features], SRC_Z)
    for peer in x_peers:
        put(src_full.at[halfs], src_full.at[halfs], SRC, peer)
    await_recv(tgt_blocks.at[0, 0], TGT_Z2)
    at = y * 4 + lax.rem(depth + 2, 4)
    for peer in y_peers:
        put(tgt_blocks.at[core_id, at], tgt_blocks.at[core_id, at], TGT_Y2, peer)

    copy_s.wait()
    await_recv(src_full.at[0 : features * (n_col - 2)], SRC)
    await_recv(tgt_blocks.at[0, 0 : 3 * (n_y - 1)], TGT_Y)
    await_recv(tgt_blocks.at[0, 0 : n_y - 1], TGT_Y2)
    put(tgt_blocks.at[core_id], tgt_blocks.at[core_id], TGT_C, pair_peer)
    feature_major(src_full, xs)
    copy_w.wait()

    def panel_strip(n, carry):
        cols = pl.ds(pl.multiple_of(n * 256, 256), 256)
        panel[:, cols] = jnp.dot(xs[256:400, :], weights[:, cols], preferred_element_type=F32)
        return carry

    lax.fori_loop(0, cols_here // 256, panel_strip, 0)

    await_recv(tgt_blocks.at[0], TGT_C)
    for k in range(n_chip):
        tgt_full[8 * k : 8 * k + 8, :] = jnp.concatenate([tgt_blocks[0, k], tgt_blocks[1, k]], axis=0)
    feature_major(tgt_full, ys)

    part = jnp.zeros((144, 256), F32)
    whole = panel[...]
    for _ in range(3):
        term = whole.astype(BF16)
        whole = whole - term.astype(F32)
        part = part + lax.dot_general(
            term, ys[256:512, :], (((1,), (1,)), ((), ())), preferred_element_type=F32
        )
    at8 = lax.broadcasted_iota(jnp.int32, (8, 128), 0)
    lane8 = lax.broadcasted_iota(jnp.int32, (8, 128), 1)
    edge = jnp.where(at8 < 2, part[128:136, 0:128], 0.0)
    corner = part[128:136, 128:256]
    corner = jnp.concatenate([corner[6:8], corner[0:6]], axis=0)
    edge = jnp.where((at8 >= 2) & (at8 < 4), corner, edge)
    side = jnp.where(at8 < 2, part[0:128, 128:256].T[0:8], 0.0)
    for s in range(group):
        parts[s, 0:8, :] = part[8 * s : 8 * s + 8, 0:128]
        one = edge[s : s + 1] if s < 8 else side[s - 8 : s - 7]
        parts[s, 8:16, :] = jnp.where(at8 == 0, one, 0.0)

    def slot_of(peer):
        return lax.rem(peer[0], 2) * n_col + peer[1]

    for peer in group_peers:
        put(parts.at[slot_of(peer)], gathered.at[slot], SCATTER, peer)
    gathered[slot] = parts[slot]
    state_major(src_full, xt)
    await_recv(gathered.at[0 : group - 1], SCATTER)
    total = gathered[0]
    for k in range(1, group):
        total = total + gathered[k]
    middle[chip] = total
    for peer in chip_peers:
        put(middle.at[chip], middle.at[chip], MIDDLE, peer)
    state_major(tgt_full, yt)
    down_rows(prior_ref[...] * (LOG2E / EPSILON), pot)
    await_recv(middle.at[0 : n_chip - 1], MIDDLE)
    total = middle[0]
    for k in range(1, n_chip):
        total = total + middle[k]
    core[slot] = total
    for peer in group_peers:
        put(core.at[slot], core.at[slot], SPREAD, peer)
    await_recv(core.at[0 : group - 1], SPREAD)

    scale = -2.0 * LOG2E / (EPSILON * total_src * total_tgt)
    main = jnp.concatenate([core[s, 0:8, :] for s in range(group)], axis=0) * (4.0 * scale)
    src_q, src_one = core[0, 8:9, :], core[1, 8:9, :]
    corner_q, corner_one = core[2, 8:9, :], core[3, 8:9, :]
    tgt_q, tgt_one = core[8, 8:9, :], core[9, 8:9, :]

    def pattern(at, first, second):
        value = jnp.where((at == 0) | (at == 2) | (at == 4), first, 0.0)
        return jnp.where((at == 1) | (at == 5), second, value)

    at16 = lax.broadcasted_iota(jnp.int32, (128, 128), 0)
    lane16 = lax.broadcasted_iota(jnp.int32, (128, 128), 1)
    lower_left = pattern(at16, src_one, src_q) * (-2.0 * scale)
    upper_right = pattern(at16, tgt_one, tgt_q).T * (-2.0 * scale)
    lower_right = pattern(
        at16,
        pattern(lane16, corner_one[:, 1:2], corner_one[:, 0:1]),
        pattern(lane16, corner_q[:, 1:2], corner_q[:, 0:1]),
    ) * scale
    left = jnp.concatenate([main, lower_left], axis=0)
    right = jnp.concatenate([upper_right, lower_right], axis=0)
    left_high, left_low = split(left)
    right_high, right_low = split(right)
    right_lane = lax.broadcasted_iota(jnp.int32, (256, 128), 1)
    ext = jnp.where(right_lane < 4, right_high.astype(F32), right_low.astype(F32)).astype(BF16)
    factor = jnp.concatenate([left_high, left_high, left_low, ext], axis=1)

    def factor_t(b, carry):
        at = pl.ds(pl.multiple_of(b * 256, 256), 256)
        u = lax.dot_general(yt[at, :], factor, (((1,), (1,)), ((), ())), preferred_element_type=F32)
        high, low = split(u[:, 0:128])
        ut[at, 0:128] = high
        ut[at, 128:256] = high
        ut[at, 256:384] = low
        high, low = split(u[:, 128:256])
        lane = lax.broadcasted_iota(jnp.int32, (256, 128), 1)
        ut[at, 384:512] = jnp.where(lane < 4, high.astype(F32), low.astype(F32)).astype(BF16)
        return carry

    lax.fori_loop(0, cols_here // 256, factor_t, 0)

    def row_strip(n, carry):
        lanes = pl.ds(pl.multiple_of(n * STRIP, STRIP), STRIP)
        cost_t[:, lanes] = jnp.dot(ut[...], xs[:, lanes], preferred_element_type=F32)
        reduce_strip(n, pot, cost_t, local)
        return carry

    lax.fori_loop(0, rows_here // STRIP, row_strip, 0)

    def make_cost():
        def factor_n(b, carry):
            cols = pl.ds(pl.multiple_of(b * 256, 256), 256)
            u = jnp.dot(factor, ys[:, cols], preferred_element_type=F32)
            high, low = split(u[0:128])
            us[0:128, cols] = high
            us[128:256, cols] = high
            us[256:384, cols] = low
            high, low = split(u[128:256])
            at = lax.broadcasted_iota(jnp.int32, (128, 256), 0)
            us[384:512, cols] = jnp.where(at < 4, high.astype(F32), low.astype(F32)).astype(BF16)
            lanes = cols
            cost[:, lanes] = jnp.dot(xt[...], us[:, lanes], preferred_element_type=F32)
            return carry

        lax.fori_loop(0, cols_here // 256, factor_n, 0)

    def strip_pass(cost_ref):
        def body(n, carry):
            reduce_strip(n, pot, cost_ref, local)
            return carry

        lax.fori_loop(0, cost_ref.shape[1] // STRIP, body, 0)

    for sweep in range(SWEEPS):
        if sweep:
            strip_pass(cost_t)
        by_col[sweep, col] = local[...]
        for peer in col_peers:
            put(by_col.at[sweep, col], by_col.at[sweep, col], ROWS + sweep, peer)
        if sweep == 0:
            make_cost()
        await_recv(by_col.at[sweep, 0 : n_col - 1], ROWS + sweep)
        f = -math.log2(total_src) - combine(by_col.at[sweep])
        down_rows(f, pot)
        strip_pass(cost)
        by_pair[sweep, core_id] = local[...]
        put(by_pair.at[sweep, core_id], by_pair.at[sweep, core_id], PAIR + sweep, pair_peer)
        await_recv(by_pair.at[sweep, 0], PAIR + sweep)
        by_chip[sweep, chip] = combine(by_pair.at[sweep])
        for peer in chip_peers:
            put(by_chip.at[sweep, chip], by_chip.at[sweep, chip], CHIPS + sweep, peer)
        await_recv(by_chip.at[sweep, 0 : n_chip - 1], CHIPS + sweep)
        g = -math.log2(total_tgt) - combine(by_chip.at[sweep])
        if sweep + 1 < SWEEPS:
            down_rows(g, pot)
    f_ref[...] = f * (EPSILON / LOG2E)
    g_ref[...] = g * (EPSILON / LOG2E)

    await_send(src_full.at[0:features], SRC_Z)
    await_send(src_full.at[0 : features * (n_col - 2)], SRC)
    await_send(tgt_blocks.at[0, 0:2], TGT_Z)
    await_send(tgt_blocks.at[0, 0], TGT_Z2)
    await_send(tgt_blocks.at[0, 0 : 3 * (n_y - 1)], TGT_Y)
    await_send(tgt_blocks.at[0, 0 : n_y - 1], TGT_Y2)
    await_send(tgt_blocks.at[0], TGT_C)
    await_send(gathered.at[0 : group - 1], SCATTER)
    await_send(middle.at[0 : n_chip - 1], MIDDLE)
    await_send(core.at[0 : group - 1], SPREAD)
    for sweep in range(SWEEPS):
        await_send(by_col.at[sweep, 0 : n_col - 1], ROWS + sweep)
        await_send(by_pair.at[sweep, 0], PAIR + sweep)
        await_send(by_chip.at[sweep, 0 : n_chip - 1], CHIPS + sweep)


def solution(mesh):
    n_row, n_col = mesh.shape["row"], mesh.shape["col"]
    n_chip = n_row // 2
    group = 2 * n_col

    def local(src_pos, tgt_pos, coupling, prior_tgt):
        rows, cols = coupling.shape
        vmem = pl.BlockSpec(memory_space=pltpu.VMEM)
        anywhere = pl.BlockSpec(memory_space=pl.ANY)
        f, g = pl.pallas_call(
            lambda *refs: kernel(n_row, n_col, *refs),
            out_shape=[
                jax.ShapeDtypeStruct((rows // 128, 128), F32),
                jax.ShapeDtypeStruct((cols // 128, 128), F32),
            ],
            in_specs=[anywhere, anywhere, anywhere, vmem],
            out_specs=[vmem, vmem],
            scratch_shapes=[
                pltpu.VMEM((rows, cols), BF16),
                pltpu.VMEM((128, rows), F32),
                pltpu.VMEM((2, n_chip, 4, cols), F32),
                pltpu.VMEM((128, cols), F32),
                pltpu.VMEM((512, rows), BF16),
                pltpu.VMEM((rows, 512), BF16),
                pltpu.VMEM((512, cols), BF16),
                pltpu.VMEM((cols, 512), BF16),
                pltpu.VMEM((512, cols), BF16),
                pltpu.VMEM((cols, 512), BF16),
                pltpu.VMEM((144, cols), F32),
                pltpu.VMEM((group, 16, 128), F32),
                pltpu.VMEM((group, 16, 128), F32),
                pltpu.VMEM((n_chip, 16, 128), F32),
                pltpu.VMEM((group, 16, 128), F32),
                pltpu.VMEM((rows, cols), F32),
                pltpu.VMEM((cols, rows), F32),
                pltpu.VMEM((max(rows, cols), 128), F32),
                pltpu.VMEM((max(rows, cols) // 128, 128), F32),
                pltpu.VMEM((SWEEPS, n_col, rows // 128, 128), F32),
                pltpu.VMEM((SWEEPS, 2, cols // 128, 128), F32),
                pltpu.VMEM((SWEEPS, n_chip, cols // 128, 128), F32),
                pltpu.SemaphoreType.DMA((19,)),
                pltpu.SemaphoreType.DMA((19,)),
            ],
            compiler_params=pltpu.CompilerParams(
                collective_id=0, has_side_effects=True, vmem_limit_bytes=63 * 2**20
            ),
        )(src_pos, tgt_pos, coupling, prior_tgt.reshape(cols // 128, 128))
        return f.reshape(rows), g.reshape(cols)

    placed = (P("col", "row"), P("row", "col"), P("row", "col"), P("col"))
    return jax.shard_map(
        local, mesh=mesh, in_specs=placed, out_specs=(P("row"), P("col")), check_vma=False
    )
```

```python
import math

import jax
import jax.numpy as jnp
from jax import lax
from jax.experimental import pallas as pl
from jax.experimental.pallas import tpu as pltpu
from jax.sharding import PartitionSpec as P

SWEEPS = 2
EPSILON = 0.25
LOG2E = 1.4426950408889634
MESH = pl.DeviceIdType.MESH
F32 = jnp.float32
BF16 = jnp.bfloat16
LOW = -3.0e38

TGT_Z, TGT_Z2, TGT_Y, TGT_Y2, TGT_C, SCATTER, MIDDLE, SPREAD, LOCAL_W, LOCAL_S, LOCAL_T = range(11)
SRC, SRC_Z, ROWS, PAIR, CHIPS = 11, 13, 15, 19, 21
SLOTS = 23


def split(value):
    high = value.astype(BF16)
    return high, (value - high.astype(F32)).astype(BF16)


def extension(x, shape, axis):
    q = jnp.sum(x * x, axis=axis, keepdims=True)
    q_high = q.astype(BF16).astype(F32)
    at = lax.broadcasted_iota(jnp.int32, shape, axis)
    ext = jnp.where((at == 1) | (at == 5), 1.0, 0.0)
    ext = jnp.where((at == 0) | (at == 4), q_high, ext)
    return jnp.where(at == 2, q - q_high, ext).astype(BF16)


def source_right(x_ref, stack, first, size):
    def block(b, carry):
        cols = pl.ds(pl.multiple_of(first + b * 512, 512), 512)
        x = x_ref[:, cols]
        stack[0:128, cols] = x.astype(BF16)
        stack[128:144, cols] = extension(x, (16, 512), 0)
        return carry

    lax.fori_loop(0, size // 512, block, 0)


def feature_major(x_ref, stack):
    def block(b, carry):
        cols = pl.ds(pl.multiple_of(b * 512, 512), 512)
        x = x_ref[:, cols]
        high, low = split(x)
        stack[0:128, cols] = high
        stack[128:256, cols] = low
        stack[256:384, cols] = high
        stack[384:400, cols] = extension(x, (16, 512), 0)
        stack[400:512, cols] = jnp.zeros((112, 512), BF16)
        return carry

    lax.fori_loop(0, x_ref.shape[1] // 512, block, 0)


def state_major(x_ref, stack):
    size = x_ref.shape[1]

    def block(b, carry):
        at = pl.ds(pl.multiple_of(b * 128, 128), 128)
        x = x_ref[:, at].T
        high, low = split(x)
        stack[at, 0:128] = high
        stack[at, 128:256] = low
        stack[at, 256:384] = high
        stack[at, 384:512] = extension(x, (128, 128), 1)
        return carry

    lax.fori_loop(0, size // 128, block, 0)


def down_rows(vector, out, first):
    for b in range(vector.shape[0]):
        at = first + 128 * b
        out[at : at + 128, :] = jnp.broadcast_to(vector[b : b + 1, :], (128, 128)).T


def tree(op, terms):
    while len(terms) > 1:
        terms = [op(*terms[k : k + 2]) if k + 1 < len(terms) else terms[k] for k in range(0, len(terms), 2)]
    return terms[0]


def row_block(at, pot, cost):
    n = cost.shape[1] // 128
    pieces = []
    for q in range(16):
        rows = pl.ds(pl.multiple_of(at + 8 * q, 8), 8)
        values = [pot[t : t + 1, :] - cost[rows, 128 * t : 128 * (t + 1)] for t in range(n)]
        top = tree(jnp.maximum, values)
        summed = tree(jnp.add, [jnp.exp2(v - top) for v in values])
        highest = jnp.max(top, axis=1, keepdims=True)
        total = jnp.sum(summed * jnp.exp2(top - highest), axis=1, keepdims=True)
        pieces.append(highest + LOG2E * jnp.log(total))
    column = jnp.concatenate(pieces, axis=0)
    eye = lax.broadcasted_iota(jnp.int32, (128, 128), 0) == lax.broadcasted_iota(jnp.int32, (128, 128), 1)
    return jnp.sum(jnp.where(eye, column, 0.0), axis=0, keepdims=True)


CHUNK = 128
STRIP = 256


def col_strip(n, first, size, pot, cost, tops, sums, out):
    lanes = pl.ds(pl.multiple_of(n * STRIP, STRIP), STRIP)

    def chunk(k, carry):
        top, summed = carry
        rows = pl.ds(pl.multiple_of(first + k * CHUNK, CHUNK), CHUNK)
        p = pot[rows, :]
        values = jnp.concatenate([p] * (STRIP // 128), axis=1) - cost[rows, lanes]
        values = values.reshape(CHUNK // 8, 8, STRIP)
        now = jnp.maximum(top, jnp.max(values, axis=0))
        summed = summed * jnp.exp2(top - now) + jnp.sum(jnp.exp2(values - now[None]), axis=0)
        return now, summed

    if first == 0:
        start = (jnp.full((8, STRIP), LOW, F32), jnp.zeros((8, STRIP), F32))
    else:
        start = (tops[:, lanes], sums[:, lanes])
    top, summed = lax.fori_loop(0, size // CHUNK, chunk, start, unroll=4)
    if out is None:
        tops[:, lanes] = top
        sums[:, lanes] = summed
        return
    highest = jnp.max(top, axis=0, keepdims=True)
    total = jnp.sum(summed * jnp.exp2(top - highest), axis=0, keepdims=True)
    result = highest + LOG2E * jnp.log(total)
    for t in range(STRIP // 128):
        out[pl.ds(n * (STRIP // 128) + t, 1), :] = result[:, 128 * t : 128 * (t + 1)]


def combine(buffer):
    n = buffer.shape[0]
    top = buffer[0]
    for k in range(1, n):
        top = jnp.maximum(top, buffer[k])
    total = jnp.exp2(buffer[0] - top)
    for k in range(1, n):
        total = total + jnp.exp2(buffer[k] - top)
    return top + LOG2E * jnp.log(total)


def kernel(
    n_row, n_col, src_ref, tgt_ref, coupling_ref, prior_ref, f_ref, g_ref,
    weights, src_full, tgt_blocks, tgt_full, xs, xt, ys, us, panel,
    parts, gathered, middle, core, cost, pot, pot_tgt, tops, sums, by_col, by_pair, by_chip,
    send, recv,
):
    row, col = lax.axis_index("row"), lax.axis_index("col")
    core_id = lax.rem(row, 2)
    chip = row // 2
    n_chip = n_row // 2
    depth = lax.rem(chip, 4)
    y = chip // 4
    n_y = n_chip // 4
    sib = row + 1 - 2 * core_id
    rows_here, cols_here = coupling_ref.shape
    total_src, total_tgt = rows_here * n_row, cols_here * n_col
    group = 2 * n_col
    slot = core_id * n_col + col

    x_size = n_col // 2
    x_at, plane_half = lax.rem(col, x_size), col // x_size
    half_col = (1 - plane_half) * x_size + x_at
    x_peers = [(row, plane_half * x_size + lax.rem(x_at + d, x_size)) for d in range(1, x_size)]
    half_peer = (row, half_col)
    z_near = [((y * 4 + lax.rem(depth + d, 4)) * 2 + core_id, col) for d in (1, 3)]
    z_far = ((y * 4 + lax.rem(depth + 2, 4)) * 2 + core_id, col)
    y_peers = [((lax.rem(y + d, n_y) * 4 + depth) * 2 + core_id, col) for d in range(1, n_y)]
    col_peers = [(row, lax.rem(col + d, n_col)) for d in range(1, n_col)]
    chip_peers = [(lax.rem(chip + d, n_chip) * 2 + core_id, col) for d in range(1, n_chip)]
    pair_peer = (sib, col)
    group_peers = col_peers + [(sib, lax.rem(col + d, n_col)) for d in range(n_col)]

    def put(source, target, index, peer):
        pltpu.make_async_remote_copy(
            src_ref=source, dst_ref=target, send_sem=send.at[index], recv_sem=recv.at[index],
            device_id=peer, device_id_type=MESH,
        ).start()

    def await_recv(ref, index):
        pltpu.make_async_copy(ref, ref, recv.at[index]).wait()

    def await_send(ref, index):
        pltpu.make_async_copy(ref, ref, send.at[index]).wait()

    barrier = pltpu.get_barrier_semaphore()
    greeted = x_peers + y_peers + z_near + [half_peer, pair_peer]
    for peer in greeted:
        pl.semaphore_signal(barrier, inc=1, device_id=peer, device_id_type=MESH)
    features = src_ref.shape[0]
    mine = pl.ds(pl.multiple_of(col * features, features), features)
    halfs = pl.ds(pl.multiple_of(half_col * features, features), features)
    copy_w = pltpu.make_async_copy(coupling_ref, weights, recv.at[LOCAL_W])
    copy_s = pltpu.make_async_copy(src_ref, src_full.at[mine], recv.at[LOCAL_S])
    copy_t = pltpu.make_async_copy(tgt_ref, tgt_blocks.at[core_id, chip], recv.at[LOCAL_T])
    copy_t.start()
    copy_s.start()
    copy_w.start()
    pl.semaphore_wait(barrier, len(greeted))

    for peer in z_near:
        put(tgt_ref, tgt_blocks.at[core_id, chip], TGT_Z, peer)
    half = rows_here // 2
    halves = [slice(0, half), slice(half, rows_here)]
    for h, cols in enumerate(halves):
        put(src_ref.at[:, cols], src_full.at[mine, cols], SRC_Z + h, half_peer)
        for peer in x_peers:
            put(src_ref.at[:, cols], src_full.at[mine, cols], SRC + h, peer)
    copy_t.wait()
    await_recv(tgt_blocks.at[0, 0:2], TGT_Z)
    put(tgt_ref, tgt_blocks.at[core_id, chip], TGT_Z2, z_far)
    for d in (0, 1, 3):
        at = y * 4 + lax.rem(depth + d, 4)
        for peer in y_peers:
            put(tgt_blocks.at[core_id, at], tgt_blocks.at[core_id, at], TGT_Y, peer)
    for h, cols in enumerate(halves):
        await_recv(src_full.at[0:features, cols], SRC_Z + h)
        for peer in x_peers:
            put(src_full.at[halfs, cols], src_full.at[halfs, cols], SRC + h, peer)
    await_recv(tgt_blocks.at[0, 0], TGT_Z2)
    at = y * 4 + lax.rem(depth + 2, 4)
    for peer in y_peers:
        put(tgt_blocks.at[core_id, at], tgt_blocks.at[core_id, at], TGT_Y2, peer)

    copy_s.wait()
    copy_w.wait()

    def panel_part(cols, more):
        def panel_strip(n, carry):
            at = pl.ds(pl.multiple_of(n * 256, 256), 256)
            term = jnp.dot(xs[:, cols], weights[cols, at], preferred_element_type=F32)
            panel[:, at] = panel[:, at] + term if more else term
            return carry

        lax.fori_loop(0, cols_here // 256, panel_strip, 0)

    await_recv(src_full.at[0 : features * (n_col - 2), halves[0]], SRC)
    source_right(src_full, xs, 0, half)
    panel_part(halves[0], False)
    await_recv(tgt_blocks.at[0, 0 : 3 * (n_y - 1)], TGT_Y)
    await_recv(tgt_blocks.at[0, 0 : n_y - 1], TGT_Y2)
    put(tgt_blocks.at[core_id], tgt_blocks.at[core_id], TGT_C, pair_peer)
    await_recv(src_full.at[0 : features * (n_col - 2), halves[1]], SRC + 1)
    source_right(src_full, xs, half, half)
    panel_part(halves[1], True)
    await_recv(tgt_blocks.at[0], TGT_C)
    for k in range(n_chip):
        tgt_full[8 * k : 8 * k + 8, :] = jnp.concatenate([tgt_blocks[0, k], tgt_blocks[1, k]], axis=0)
    feature_major(tgt_full, ys)

    part = jnp.zeros((144, 256), F32)
    whole = panel[...]
    for _ in range(3):
        term = whole.astype(BF16)
        whole = whole - term.astype(F32)
        part = part + lax.dot_general(
            term, ys[256:512, :], (((1,), (1,)), ((), ())), preferred_element_type=F32
        )
    at8 = lax.broadcasted_iota(jnp.int32, (8, 128), 0)
    lane8 = lax.broadcasted_iota(jnp.int32, (8, 128), 1)
    edge = jnp.where(at8 < 2, part[128:136, 0:128], 0.0)
    corner = part[128:136, 128:256]
    corner = jnp.concatenate([corner[6:8], corner[0:6]], axis=0)
    edge = jnp.where((at8 >= 2) & (at8 < 4), corner, edge)
    side = jnp.where(at8 < 2, part[0:128, 128:256].T[0:8], 0.0)
    for s in range(group):
        parts[s, 0:8, :] = part[8 * s : 8 * s + 8, 0:128]
        one = edge[s : s + 1] if s < 8 else side[s - 8 : s - 7]
        parts[s, 8:16, :] = jnp.where(at8 == 0, one, 0.0)

    def slot_of(peer):
        return lax.rem(peer[0], 2) * n_col + peer[1]

    for peer in group_peers:
        put(parts.at[slot_of(peer)], gathered.at[slot], SCATTER, peer)
    gathered[slot] = parts[slot]
    state_major(src_full, xt)
    await_recv(gathered.at[0 : group - 1], SCATTER)
    total = gathered[0]
    for k in range(1, group):
        total = total + gathered[k]
    middle[chip] = total
    for peer in chip_peers:
        put(middle.at[chip], middle.at[chip], MIDDLE, peer)
    pot_tgt[...] = prior_ref[...] * (LOG2E / EPSILON)
    await_recv(middle.at[0 : n_chip - 1], MIDDLE)
    total = middle[0]
    for k in range(1, n_chip):
        total = total + middle[k]
    core[slot] = total
    for peer in group_peers:
        put(core.at[slot], core.at[slot], SPREAD, peer)
    await_recv(core.at[0 : group - 1], SPREAD)

    scale = -2.0 * LOG2E / (EPSILON * total_src * total_tgt)
    main = jnp.concatenate([core[s, 0:8, :] for s in range(group)], axis=0) * (4.0 * scale)
    src_q, src_one = core[0, 8:9, :], core[1, 8:9, :]
    corner_q, corner_one = core[2, 8:9, :], core[3, 8:9, :]
    tgt_q, tgt_one = core[8, 8:9, :], core[9, 8:9, :]

    def pattern(at, first, second):
        value = jnp.where((at == 0) | (at == 2) | (at == 4), first, 0.0)
        return jnp.where((at == 1) | (at == 5), second, value)

    at16 = lax.broadcasted_iota(jnp.int32, (128, 128), 0)
    lane16 = lax.broadcasted_iota(jnp.int32, (128, 128), 1)
    lower_left = pattern(at16, src_one, src_q) * (-2.0 * scale)
    upper_right = pattern(at16, tgt_one, tgt_q).T * (-2.0 * scale)
    lower_right = pattern(
        at16,
        pattern(lane16, corner_one[:, 1:2], corner_one[:, 0:1]),
        pattern(lane16, corner_q[:, 1:2], corner_q[:, 0:1]),
    ) * scale
    left = jnp.concatenate([main, lower_left], axis=0)
    right = jnp.concatenate([upper_right, lower_right], axis=0)
    left_high, left_low = split(left)
    right_high, right_low = split(right)
    right_lane = lax.broadcasted_iota(jnp.int32, (256, 128), 1)
    ext = jnp.where(right_lane < 4, right_high.astype(F32), right_low.astype(F32)).astype(BF16)
    factor = jnp.concatenate([left_high, left_high, left_low, ext], axis=1)

    def factor_strip(n):
        cols = pl.ds(pl.multiple_of(n * 256, 256), 256)
        u = jnp.dot(factor, ys[:, cols], preferred_element_type=F32)
        high, low = split(u[0:128])
        us[0:128, cols] = high
        us[128:256, cols] = high
        us[256:384, cols] = low
        high, low = split(u[128:256])
        at = lax.broadcasted_iota(jnp.int32, (128, 256), 0)
        us[384:512, cols] = jnp.where(at < 4, high.astype(F32), low.astype(F32)).astype(BF16)

    n_strips = cols_here // 256

    def cost_strip(n, carry):
        lanes = pl.ds(pl.multiple_of(n * 256, 256), 256)
        cost[:, lanes] = jnp.dot(xt[...], us[:, lanes], preferred_element_type=F32)
        return carry

    def factor_loop(n, carry):
        factor_strip(n)
        return carry

    lax.fori_loop(0, n_strips, factor_loop, 0)
    lax.fori_loop(0, n_strips, cost_strip, 0)

    n_part = half // 128
    for sweep in range(SWEEPS):
        for h in range(2):
            mine_now = by_col.at[sweep, h, col]

            def block(b, carry):
                mine_now[pl.ds(b, 1), :] = row_block(h * half + b * 128, pot_tgt, cost)
                return carry

            lax.fori_loop(0, n_part, block, 0)
            for peer in col_peers:
                put(mine_now, mine_now, ROWS + 2 * sweep + h, peer)
        f = []
        for h in range(2):
            await_recv(by_col.at[sweep, h, 0 : n_col - 1], ROWS + 2 * sweep + h)
            f.append(-math.log2(total_src) - combine(by_col.at[sweep, h]))
            down_rows(f[h], pot, h * half)
            out = by_pair.at[sweep, core_id] if h else None

            def strip(n, carry):
                col_strip(n, h * half, half, pot, cost, tops, sums, out)
                return carry

            lax.fori_loop(0, cols_here // STRIP, strip, 0)
        put(by_pair.at[sweep, core_id], by_pair.at[sweep, core_id], PAIR + sweep, pair_peer)
        await_recv(by_pair.at[sweep, 0], PAIR + sweep)
        by_chip[sweep, chip] = combine(by_pair.at[sweep])
        for peer in chip_peers:
            put(by_chip.at[sweep, chip], by_chip.at[sweep, chip], CHIPS + sweep, peer)
        await_recv(by_chip.at[sweep, 0 : n_chip - 1], CHIPS + sweep)
        g = -math.log2(total_tgt) - combine(by_chip.at[sweep])
        pot_tgt[...] = g
    f_ref[...] = jnp.concatenate(f, axis=0) * (EPSILON / LOG2E)
    g_ref[...] = g * (EPSILON / LOG2E)

    for h, cols in enumerate(halves):
        await_send(src_full.at[0:features, cols], SRC_Z + h)
        await_send(src_full.at[0 : features * (n_col - 2), cols], SRC + h)
    await_send(tgt_blocks.at[0, 0:2], TGT_Z)
    await_send(tgt_blocks.at[0, 0], TGT_Z2)
    await_send(tgt_blocks.at[0, 0 : 3 * (n_y - 1)], TGT_Y)
    await_send(tgt_blocks.at[0, 0 : n_y - 1], TGT_Y2)
    await_send(tgt_blocks.at[0], TGT_C)
    await_send(gathered.at[0 : group - 1], SCATTER)
    await_send(middle.at[0 : n_chip - 1], MIDDLE)
    await_send(core.at[0 : group - 1], SPREAD)
    for sweep in range(SWEEPS):
        for h in range(2):
            await_send(by_col.at[sweep, h, 0 : n_col - 1], ROWS + 2 * sweep + h)
        await_send(by_pair.at[sweep, 0], PAIR + sweep)
        await_send(by_chip.at[sweep, 0 : n_chip - 1], CHIPS + sweep)


def solution(mesh):
    n_row, n_col = mesh.shape["row"], mesh.shape["col"]
    n_chip = n_row // 2
    group = 2 * n_col

    def local(src_pos, tgt_pos, coupling, prior_tgt):
        rows, cols = coupling.shape
        vmem = pl.BlockSpec(memory_space=pltpu.VMEM)
        anywhere = pl.BlockSpec(memory_space=pl.ANY)
        f, g = pl.pallas_call(
            lambda *refs: kernel(n_row, n_col, *refs),
            out_shape=[
                jax.ShapeDtypeStruct((rows // 128, 128), F32),
                jax.ShapeDtypeStruct((cols // 128, 128), F32),
            ],
            in_specs=[anywhere, anywhere, anywhere, vmem],
            out_specs=[vmem, vmem],
            scratch_shapes=[
                pltpu.VMEM((rows, cols), BF16),
                pltpu.VMEM((128, rows), F32),
                pltpu.VMEM((2, n_chip, 4, cols), F32),
                pltpu.VMEM((128, cols), F32),
                pltpu.VMEM((144, rows), BF16),
                pltpu.VMEM((rows, 512), BF16),
                pltpu.VMEM((512, cols), BF16),
                pltpu.VMEM((512, cols), BF16),
                pltpu.VMEM((144, cols), F32),
                pltpu.VMEM((group, 16, 128), F32),
                pltpu.VMEM((group, 16, 128), F32),
                pltpu.VMEM((n_chip, 16, 128), F32),
                pltpu.VMEM((group, 16, 128), F32),
                pltpu.VMEM((rows, cols), F32),
                pltpu.VMEM((rows, 128), F32),
                pltpu.VMEM((cols // 128, 128), F32),
                pltpu.VMEM((8, cols), F32),
                pltpu.VMEM((8, cols), F32),
                pltpu.VMEM((SWEEPS, 2, n_col, rows // 256, 128), F32),
                pltpu.VMEM((SWEEPS, 2, cols // 128, 128), F32),
                pltpu.VMEM((SWEEPS, n_chip, cols // 128, 128), F32),
                pltpu.SemaphoreType.DMA((SLOTS,)),
                pltpu.SemaphoreType.DMA((SLOTS,)),
            ],
            compiler_params=pltpu.CompilerParams(
                collective_id=0, has_side_effects=True, vmem_limit_bytes=63 * 2**20
            ),
        )(src_pos, tgt_pos, coupling, prior_tgt.reshape(cols // 128, 128))
        return f.reshape(rows), g.reshape(cols)

    placed = (P("col", "row"), P("row", "col"), P("row", "col"), P("col"))
    return jax.shard_map(
        local, mesh=mesh, in_specs=placed, out_specs=(P("row"), P("col")), check_vma=False
    )
```

```python
import math

import jax
import jax.numpy as jnp
from jax import lax
from jax.experimental import pallas as pl
from jax.experimental.pallas import tpu as pltpu
from jax.sharding import PartitionSpec as P

SWEEPS = 2
EPSILON = 0.25
LOG2E = 1.4426950408889634
MESH = pl.DeviceIdType.MESH
F32 = jnp.float32
BF16 = jnp.bfloat16
LOW = -3.0e38

TGT_Z, TGT_Z2, TGT_Y, TGT_Y2, TGT_C, SCATTER, MIDDLE, SPREAD, LOCAL_W, LOCAL_S, LOCAL_T = range(11)
SRC_Z, ROWS, PAIR, CHIPS, NEAR, FAR = 11, 13, 17, 19, 21, 29
SLOTS = 33


def split(value):
    high = value.astype(BF16)
    return high, (value - high.astype(F32)).astype(BF16)


def extension(x, shape, axis):
    q = jnp.sum(x * x, axis=axis, keepdims=True)
    q_high = q.astype(BF16).astype(F32)
    at = lax.broadcasted_iota(jnp.int32, shape, axis)
    ext = jnp.where((at == 1) | (at == 5), 1.0, 0.0)
    ext = jnp.where((at == 0) | (at == 4), q_high, ext)
    return jnp.where(at == 2, q - q_high, ext).astype(BF16)


def source_right(x_ref, stack, first, size):
    def block(b, carry):
        cols = pl.ds(pl.multiple_of(first + b * 512, 512), 512)
        x = x_ref[:, cols]
        stack[0:128, cols] = x.astype(BF16)
        stack[128:144, cols] = extension(x, (16, 512), 0)
        return carry

    lax.fori_loop(0, size // 512, block, 0)


def feature_major(x_ref, stack):
    def block(b, carry):
        cols = pl.ds(pl.multiple_of(b * 512, 512), 512)
        x = x_ref[:, cols]
        high, low = split(x)
        stack[0:128, cols] = high
        stack[128:256, cols] = low
        stack[256:384, cols] = high
        stack[384:400, cols] = extension(x, (16, 512), 0)
        stack[400:512, cols] = jnp.zeros((112, 512), BF16)
        return carry

    lax.fori_loop(0, x_ref.shape[1] // 512, block, 0)


def state_major(x_ref, stack):
    size = x_ref.shape[1]

    def block(b, carry):
        at = pl.ds(pl.multiple_of(b * 128, 128), 128)
        x = x_ref[:, at].T
        high, low = split(x)
        stack[at, 0:128] = high
        stack[at, 128:256] = low
        stack[at, 256:384] = high
        stack[at, 384:512] = extension(x, (128, 128), 1)
        return carry

    lax.fori_loop(0, size // 128, block, 0)


def down_rows(vector, out, first):
    for b in range(vector.shape[0]):
        at = first + 128 * b
        out[at : at + 128, :] = jnp.broadcast_to(vector[b : b + 1, :], (128, 128)).T


def tree(op, terms):
    while len(terms) > 1:
        terms = [op(*terms[k : k + 2]) if k + 1 < len(terms) else terms[k] for k in range(0, len(terms), 2)]
    return terms[0]


def row_partial(at, pot, cost, tops, sums):
    rows = pl.ds(pl.multiple_of(at, 8), 8)
    values = [pot[t : t + 1, :] - cost[rows, 128 * t : 128 * (t + 1)] for t in range(cost.shape[1] // 128)]
    top = tree(jnp.maximum, values)
    tops[rows, :] = top
    sums[rows, :] = tree(jnp.add, [jnp.exp2(v - top) for v in values])


def row_finish(at, tops, sums):
    top = tops[at : at + 128, :].T
    highest = jnp.max(top, axis=0, keepdims=True)
    total = jnp.sum(sums[at : at + 128, :].T * jnp.exp2(top - highest), axis=0, keepdims=True)
    return highest + LOG2E * jnp.log(total)


CHUNK = 128
STRIP = 256


def col_strip(n, first, size, pot, cost, tops, sums, out):
    lanes = pl.ds(pl.multiple_of(n * STRIP, STRIP), STRIP)

    def chunk(k, carry):
        top, summed = carry
        rows = pl.ds(pl.multiple_of(first + k * CHUNK, CHUNK), CHUNK)
        p = pot[rows, :]
        values = jnp.concatenate([p] * (STRIP // 128), axis=1) - cost[rows, lanes]
        values = values.reshape(CHUNK // 8, 8, STRIP)
        now = jnp.maximum(top, jnp.max(values, axis=0))
        summed = summed * jnp.exp2(top - now) + jnp.sum(jnp.exp2(values - now[None]), axis=0)
        return now, summed

    if first == 0:
        start = (jnp.full((8, STRIP), LOW, F32), jnp.zeros((8, STRIP), F32))
    else:
        start = (tops[:, lanes], sums[:, lanes])
    top, summed = lax.fori_loop(0, size // CHUNK, chunk, start, unroll=4)
    if out is None:
        tops[:, lanes] = top
        sums[:, lanes] = summed
        return
    highest = jnp.max(top, axis=0, keepdims=True)
    total = jnp.sum(summed * jnp.exp2(top - highest), axis=0, keepdims=True)
    result = highest + LOG2E * jnp.log(total)
    for t in range(STRIP // 128):
        out[pl.ds(n * (STRIP // 128) + t, 1), :] = result[:, 128 * t : 128 * (t + 1)]


def combine(buffer):
    n = buffer.shape[0]
    top = buffer[0]
    for k in range(1, n):
        top = jnp.maximum(top, buffer[k])
    total = jnp.exp2(buffer[0] - top)
    for k in range(1, n):
        total = total + jnp.exp2(buffer[k] - top)
    return top + LOG2E * jnp.log(total)


def kernel(
    n_row, n_col, src_ref, tgt_ref, coupling_ref, prior_ref, f_ref, g_ref,
    weights, src_full, tgt_blocks, tgt_full, xs, xt, ys, us, panel,
    parts, gathered, middle, core, cost, pot, pot_tgt, tops, sums, row_tops, row_sums, by_col, by_pair, by_chip,
    send, recv,
):
    row, col = lax.axis_index("row"), lax.axis_index("col")
    core_id = lax.rem(row, 2)
    chip = row // 2
    n_chip = n_row // 2
    depth = lax.rem(chip, 4)
    y = chip // 4
    n_y = n_chip // 4
    sib = row + 1 - 2 * core_id
    rows_here, cols_here = coupling_ref.shape
    total_src, total_tgt = rows_here * n_row, cols_here * n_col
    group = 2 * n_col
    slot = core_id * n_col + col

    x_size = n_col // 2
    x_at, plane_half = lax.rem(col, x_size), col // x_size
    half_col = (1 - plane_half) * x_size + x_at
    next_x, last_x = lax.rem(x_at + 1, x_size), lax.rem(x_at + x_size - 1, x_size)
    x_near = [(row, plane_half * x_size + next_x), (row, plane_half * x_size + last_x)]
    half_peer = (row, half_col)
    z_near = [((y * 4 + lax.rem(depth + d, 4)) * 2 + core_id, col) for d in (1, 3)]
    z_far = ((y * 4 + lax.rem(depth + 2, 4)) * 2 + core_id, col)
    y_peers = [((lax.rem(y + d, n_y) * 4 + depth) * 2 + core_id, col) for d in range(1, n_y)]
    col_peers = [(row, lax.rem(col + d, n_col)) for d in range(1, n_col)]
    chip_peers = [(lax.rem(chip + d, n_chip) * 2 + core_id, col) for d in range(1, n_chip)]
    pair_peer = (sib, col)
    group_peers = col_peers + [(sib, lax.rem(col + d, n_col)) for d in range(n_col)]

    def put(source, target, index, peer):
        pltpu.make_async_remote_copy(
            src_ref=source, dst_ref=target, send_sem=send.at[index], recv_sem=recv.at[index],
            device_id=peer, device_id_type=MESH,
        ).start()

    def await_recv(ref, index):
        pltpu.make_async_copy(ref, ref, recv.at[index]).wait()

    def await_send(ref, index):
        pltpu.make_async_copy(ref, ref, send.at[index]).wait()

    barrier = pltpu.get_barrier_semaphore()
    greeted = x_near + y_peers + z_near + [half_peer, pair_peer]
    for peer in greeted:
        pl.semaphore_signal(barrier, inc=1, device_id=peer, device_id_type=MESH)
    features = src_ref.shape[0]
    mine = pl.ds(pl.multiple_of(col * features, features), features)
    copy_w = pltpu.make_async_copy(coupling_ref, weights, recv.at[LOCAL_W])
    copy_s = pltpu.make_async_copy(src_ref, src_full.at[mine], recv.at[LOCAL_S])
    copy_t = pltpu.make_async_copy(tgt_ref, tgt_blocks.at[core_id, chip], recv.at[LOCAL_T])
    copy_t.start()
    copy_s.start()
    copy_w.start()
    pl.semaphore_wait(barrier, len(greeted))

    for peer in z_near:
        put(tgt_ref, tgt_blocks.at[core_id, chip], TGT_Z, peer)
    half = rows_here // 2
    halves = [slice(0, half), slice(half, rows_here)]
    def block_at(c, h):
        return src_full.at[pl.ds(pl.multiple_of(c * features, features), features), halves[h]]

    def near(c, h, k, source=None):
        for d in range(2):
            put(source or block_at(c, h), block_at(c, h), NEAR + 4 * (1 - d) + 2 * k + h, x_near[d])

    def onward(h, k):
        d = 1 - h
        side = plane_half if k == 0 else 1 - plane_half
        block = block_at(side * x_size + (last_x if d else next_x), h)
        await_recv(block, NEAR + 4 * d + 2 * k + h)
        put(block, block, FAR + 2 * k + h, x_near[1 - d])

    def arrived(h):
        for k in range(2):
            await_recv(block_at(col, h), NEAR + 4 * h + 2 * k + h)
            await_recv(block_at(col, h), FAR + 2 * k + h)

    def plane_block(d):
        return tgt_blocks.at[core_id, y * 4 + lax.rem(depth + d, 4)]

    for h in range(2):
        own = src_ref.at[:, halves[h]]
        put(own, block_at(col, h), SRC_Z + h, half_peer)
        near(col, h, 0, own)
    copy_t.wait()
    await_recv(tgt_blocks.at[0, 0:2], TGT_Z)
    put(tgt_ref, tgt_blocks.at[core_id, chip], TGT_Z2, z_far)
    for d in (0, 1, 3):
        for peer in y_peers:
            put(plane_block(d), plane_block(d), TGT_Y, peer)
    await_recv(block_at(col, 0), SRC_Z)
    near(half_col, 0, 1)
    onward(0, 0)
    await_recv(block_at(col, 1), SRC_Z + 1)
    near(half_col, 1, 1)
    onward(1, 0)
    for d in (0, 1, 3):
        put(plane_block(d), plane_block(d), TGT_C, pair_peer)
    await_recv(tgt_blocks.at[0, 0], TGT_Z2)
    for peer in y_peers:
        put(plane_block(2), plane_block(2), TGT_Y2, peer)
    put(plane_block(2), plane_block(2), TGT_C, pair_peer)
    onward(0, 1)
    onward(1, 1)
    await_recv(tgt_blocks.at[0, 0 : 3 * (n_y - 1)], TGT_Y)
    for e in range(1, n_y):
        for d in (0, 1, 3):
            block = tgt_blocks.at[core_id, lax.rem(y + e, n_y) * 4 + lax.rem(depth + d, 4)]
            put(block, block, TGT_C, pair_peer)

    copy_s.wait()
    copy_w.wait()

    def panel_part(cols, more):
        def panel_strip(n, carry):
            at = pl.ds(pl.multiple_of(n * 256, 256), 256)
            term = jnp.dot(xs[:, cols], weights[cols, at], preferred_element_type=F32)
            panel[:, at] = panel[:, at] + term if more else term
            return carry

        lax.fori_loop(0, cols_here // 256, panel_strip, 0)

    arrived(0)
    source_right(src_full, xs, 0, half)
    panel_part(halves[0], False)
    await_recv(tgt_blocks.at[0, 0 : n_y - 1], TGT_Y2)
    for e in range(1, n_y):
        block = tgt_blocks.at[core_id, lax.rem(y + e, n_y) * 4 + lax.rem(depth + 2, 4)]
        put(block, block, TGT_C, pair_peer)
    arrived(1)
    source_right(src_full, xs, half, half)
    panel_part(halves[1], True)
    await_recv(tgt_blocks.at[0], TGT_C)
    for k in range(n_chip):
        tgt_full[8 * k : 8 * k + 8, :] = jnp.concatenate([tgt_blocks[0, k], tgt_blocks[1, k]], axis=0)
    feature_major(tgt_full, ys)

    part = jnp.zeros((144, 256), F32)
    whole = panel[...]
    for _ in range(3):
        term = whole.astype(BF16)
        whole = whole - term.astype(F32)
        part = part + lax.dot_general(
            term, ys[256:512, :], (((1,), (1,)), ((), ())), preferred_element_type=F32
        )
    at8 = lax.broadcasted_iota(jnp.int32, (8, 128), 0)
    lane8 = lax.broadcasted_iota(jnp.int32, (8, 128), 1)
    edge = jnp.where(at8 < 2, part[128:136, 0:128], 0.0)
    corner = part[128:136, 128:256]
    corner = jnp.concatenate([corner[6:8], corner[0:6]], axis=0)
    edge = jnp.where((at8 >= 2) & (at8 < 4), corner, edge)
    side = jnp.where(at8 < 2, part[0:128, 128:256].T[0:8], 0.0)
    for s in range(group):
        parts[s, 0:8, :] = part[8 * s : 8 * s + 8, 0:128]
        one = edge[s : s + 1] if s < 8 else side[s - 8 : s - 7]
        parts[s, 8:16, :] = jnp.where(at8 == 0, one, 0.0)

    def slot_of(peer):
        return lax.rem(peer[0], 2) * n_col + peer[1]

    for peer in group_peers:
        put(parts.at[slot_of(peer)], gathered.at[slot], SCATTER, peer)
    gathered[slot] = parts[slot]
    state_major(src_full, xt)
    await_recv(gathered.at[0 : group - 1], SCATTER)
    total = gathered[0]
    for k in range(1, group):
        total = total + gathered[k]
    middle[chip] = total
    for peer in chip_peers:
        put(middle.at[chip], middle.at[chip], MIDDLE, peer)
    pot_tgt[...] = prior_ref[...] * (LOG2E / EPSILON)
    await_recv(middle.at[0 : n_chip - 1], MIDDLE)
    total = middle[0]
    for k in range(1, n_chip):
        total = total + middle[k]
    core[slot] = total
    for peer in group_peers:
        put(core.at[slot], core.at[slot], SPREAD, peer)
    await_recv(core.at[0 : group - 1], SPREAD)

    scale = -2.0 * LOG2E / (EPSILON * total_src * total_tgt)
    main = jnp.concatenate([core[s, 0:8, :] for s in range(group)], axis=0) * (4.0 * scale)
    src_q, src_one = core[0, 8:9, :], core[1, 8:9, :]
    corner_q, corner_one = core[2, 8:9, :], core[3, 8:9, :]
    tgt_q, tgt_one = core[8, 8:9, :], core[9, 8:9, :]

    def pattern(at, first, second):
        value = jnp.where((at == 0) | (at == 2) | (at == 4), first, 0.0)
        return jnp.where((at == 1) | (at == 5), second, value)

    at16 = lax.broadcasted_iota(jnp.int32, (128, 128), 0)
    lane16 = lax.broadcasted_iota(jnp.int32, (128, 128), 1)
    lower_left = pattern(at16, src_one, src_q) * (-2.0 * scale)
    upper_right = pattern(at16, tgt_one, tgt_q).T * (-2.0 * scale)
    lower_right = pattern(
        at16,
        pattern(lane16, corner_one[:, 1:2], corner_one[:, 0:1]),
        pattern(lane16, corner_q[:, 1:2], corner_q[:, 0:1]),
    ) * scale
    left = jnp.concatenate([main, lower_left], axis=0)
    right = jnp.concatenate([upper_right, lower_right], axis=0)
    left_high, left_low = split(left)
    right_high, right_low = split(right)
    right_lane = lax.broadcasted_iota(jnp.int32, (256, 128), 1)
    ext = jnp.where(right_lane < 4, right_high.astype(F32), right_low.astype(F32)).astype(BF16)
    factor = jnp.concatenate([left_high, left_high, left_low, ext], axis=1)

    def factor_strip(n):
        cols = pl.ds(pl.multiple_of(n * 256, 256), 256)
        u = jnp.dot(factor, ys[:, cols], preferred_element_type=F32)
        high, low = split(u[0:128])
        us[0:128, cols] = high
        us[128:256, cols] = high
        us[256:384, cols] = low
        high, low = split(u[128:256])
        at = lax.broadcasted_iota(jnp.int32, (128, 256), 0)
        us[384:512, cols] = jnp.where(at < 4, high.astype(F32), low.astype(F32)).astype(BF16)

    n_strips = cols_here // 256

    def cost_strip(n, carry):
        lanes = pl.ds(pl.multiple_of(n * 256, 256), 256)
        cost[:, lanes] = jnp.dot(xt[...], us[:, lanes], preferred_element_type=F32)
        return carry

    def factor_loop(n, carry):
        factor_strip(n)
        return carry

    lax.fori_loop(0, n_strips, factor_loop, 0)
    lax.fori_loop(0, n_strips, cost_strip, 0)

    n_part = half // 128
    for sweep in range(SWEEPS):
        for h in range(2):
            mine_now = by_col.at[sweep, h, col]

            def block(b, carry):
                for q in range(8):
                    row_partial(h * half + b * 64 + 8 * q, pot_tgt, cost, row_tops, row_sums)
                return carry

            lax.fori_loop(0, half // 64, block, 0)
            for b in range(n_part):
                mine_now[b : b + 1, :] = row_finish(h * half + 128 * b, row_tops, row_sums)
            for peer in col_peers:
                put(mine_now, mine_now, ROWS + 2 * sweep + h, peer)
        f = []
        for h in range(2):
            await_recv(by_col.at[sweep, h, 0 : n_col - 1], ROWS + 2 * sweep + h)
            f.append(-math.log2(total_src) - combine(by_col.at[sweep, h]))
            down_rows(f[h], pot, h * half)
            out = by_pair.at[sweep, core_id] if h else None

            def strip(n, carry):
                col_strip(n, h * half, half, pot, cost, tops, sums, out)
                return carry

            lax.fori_loop(0, cols_here // STRIP, strip, 0)
        put(by_pair.at[sweep, core_id], by_pair.at[sweep, core_id], PAIR + sweep, pair_peer)
        await_recv(by_pair.at[sweep, 0], PAIR + sweep)
        by_chip[sweep, chip] = combine(by_pair.at[sweep])
        for peer in chip_peers:
            put(by_chip.at[sweep, chip], by_chip.at[sweep, chip], CHIPS + sweep, peer)
        await_recv(by_chip.at[sweep, 0 : n_chip - 1], CHIPS + sweep)
        g = -math.log2(total_tgt) - combine(by_chip.at[sweep])
        pot_tgt[...] = g
    f_ref[...] = jnp.concatenate(f, axis=0) * (EPSILON / LOG2E)
    g_ref[...] = g * (EPSILON / LOG2E)

    for h in range(2):
        await_send(block_at(col, h), SRC_Z + h)
        for k in range(2):
            await_send(block_at(col, h), FAR + 2 * k + h)
            for d in range(2):
                await_send(block_at(col, h), NEAR + 4 * d + 2 * k + h)
    await_send(tgt_blocks.at[0, 0:2], TGT_Z)
    await_send(tgt_blocks.at[0, 0], TGT_Z2)
    await_send(tgt_blocks.at[0, 0 : 3 * (n_y - 1)], TGT_Y)
    await_send(tgt_blocks.at[0, 0 : n_y - 1], TGT_Y2)
    await_send(tgt_blocks.at[0], TGT_C)
    await_send(gathered.at[0 : group - 1], SCATTER)
    await_send(middle.at[0 : n_chip - 1], MIDDLE)
    await_send(core.at[0 : group - 1], SPREAD)
    for sweep in range(SWEEPS):
        for h in range(2):
            await_send(by_col.at[sweep, h, 0 : n_col - 1], ROWS + 2 * sweep + h)
        await_send(by_pair.at[sweep, 0], PAIR + sweep)
        await_send(by_chip.at[sweep, 0 : n_chip - 1], CHIPS + sweep)


def solution(mesh):
    n_row, n_col = mesh.shape["row"], mesh.shape["col"]
    n_chip = n_row // 2
    group = 2 * n_col

    def local(src_pos, tgt_pos, coupling, prior_tgt):
        rows, cols = coupling.shape
        vmem = pl.BlockSpec(memory_space=pltpu.VMEM)
        anywhere = pl.BlockSpec(memory_space=pl.ANY)
        f, g = pl.pallas_call(
            lambda *refs: kernel(n_row, n_col, *refs),
            out_shape=[
                jax.ShapeDtypeStruct((rows // 128, 128), F32),
                jax.ShapeDtypeStruct((cols // 128, 128), F32),
            ],
            in_specs=[anywhere, anywhere, anywhere, vmem],
            out_specs=[vmem, vmem],
            scratch_shapes=[
                pltpu.VMEM((rows, cols), BF16),
                pltpu.VMEM((128, rows), F32),
                pltpu.VMEM((2, n_chip, 4, cols), F32),
                pltpu.VMEM((128, cols), F32),
                pltpu.VMEM((144, rows), BF16),
                pltpu.VMEM((rows, 512), BF16),
                pltpu.VMEM((512, cols), BF16),
                pltpu.VMEM((512, cols), BF16),
                pltpu.VMEM((144, cols), F32),
                pltpu.VMEM((group, 16, 128), F32),
                pltpu.VMEM((group, 16, 128), F32),
                pltpu.VMEM((n_chip, 16, 128), F32),
                pltpu.VMEM((group, 16, 128), F32),
                pltpu.VMEM((rows, cols), F32),
                pltpu.VMEM((rows, 128), F32),
                pltpu.VMEM((cols // 128, 128), F32),
                pltpu.VMEM((8, cols), F32),
                pltpu.VMEM((8, cols), F32),
                pltpu.VMEM((rows, 128), F32),
                pltpu.VMEM((rows, 128), F32),
                pltpu.VMEM((SWEEPS, 2, n_col, rows // 256, 128), F32),
                pltpu.VMEM((SWEEPS, 2, cols // 128, 128), F32),
                pltpu.VMEM((SWEEPS, n_chip, cols // 128, 128), F32),
                pltpu.SemaphoreType.DMA((SLOTS,)),
                pltpu.SemaphoreType.DMA((SLOTS,)),
            ],
            compiler_params=pltpu.CompilerParams(
                collective_id=0, has_side_effects=True, vmem_limit_bytes=63 * 2**20
            ),
        )(src_pos, tgt_pos, coupling, prior_tgt.reshape(cols // 128, 128))
        return f.reshape(rows), g.reshape(cols)

    placed = (P("col", "row"), P("row", "col"), P("row", "col"), P("col"))
    return jax.shard_map(
        local, mesh=mesh, in_specs=placed, out_specs=(P("row"), P("col")), check_vma=False
    )
```

```python
import math

import jax
import jax.numpy as jnp
from jax import lax
from jax.experimental import pallas as pl
from jax.experimental.pallas import tpu as pltpu
from jax.sharding import PartitionSpec as P

SWEEPS = 2
EPSILON = 0.25
LOG2E = 1.4426950408889634
MESH = pl.DeviceIdType.MESH
F32 = jnp.float32
BF16 = jnp.bfloat16
LOW = -3.0e38

TGT_Z, TGT_Z2, TGT_Y, TGT_Y2, TGT_C, SCATTER, MIDDLE, SPREAD, LOCAL_W, LOCAL_S, LOCAL_T = range(11)
SRC_Z, ROWS, PAIR, CHIPS, NEAR, FAR = 11, 13, 17, 19, 21, 29
SLOTS = 33


def split(value):
    high = value.astype(BF16)
    return high, (value - high.astype(F32)).astype(BF16)


def extension(x, shape, axis):
    q = jnp.sum(x * x, axis=axis, keepdims=True)
    q_high = q.astype(BF16).astype(F32)
    at = lax.broadcasted_iota(jnp.int32, shape, axis)
    ext = jnp.where((at == 1) | (at == 5), 1.0, 0.0)
    ext = jnp.where((at == 0) | (at == 4), q_high, ext)
    return jnp.where(at == 2, q - q_high, ext).astype(BF16)


def source_right(x_ref, stack, first, size):
    def block(b, carry):
        cols = pl.ds(pl.multiple_of(first + b * 512, 512), 512)
        x = x_ref[:, cols]
        stack[0:128, cols] = x.astype(BF16)
        stack[128:144, cols] = extension(x, (16, 512), 0)
        return carry

    lax.fori_loop(0, size // 512, block, 0)


def feature_major(x_ref, stack):
    def block(b, carry):
        cols = pl.ds(pl.multiple_of(b * 512, 512), 512)
        x = x_ref[:, cols]
        high, low = split(x)
        stack[0:128, cols] = high
        stack[128:256, cols] = low
        stack[256:384, cols] = high
        stack[384:400, cols] = extension(x, (16, 512), 0)
        stack[400:512, cols] = jnp.zeros((112, 512), BF16)
        return carry

    lax.fori_loop(0, x_ref.shape[1] // 512, block, 0)


def state_major(x_ref, stack):
    size = x_ref.shape[1]

    def block(b, carry):
        at = pl.ds(pl.multiple_of(b * 128, 128), 128)
        x = x_ref[:, at].T
        high, low = split(x)
        stack[at, 0:128] = high
        stack[at, 128:256] = low
        stack[at, 256:384] = high
        stack[at, 384:512] = extension(x, (128, 128), 1)
        return carry

    lax.fori_loop(0, size // 128, block, 0)


def down_rows(vector, out, first):
    for b in range(vector.shape[0]):
        at = first + 128 * b
        out[at : at + 128, :] = jnp.broadcast_to(vector[b : b + 1, :], (128, 128)).T


def tree(op, terms):
    while len(terms) > 1:
        terms = [op(*terms[k : k + 2]) if k + 1 < len(terms) else terms[k] for k in range(0, len(terms), 2)]
    return terms[0]


def row_partial(at, pot, cost, tops, sums):
    rows = pl.ds(pl.multiple_of(at, 8), 8)
    values = [pot[t : t + 1, :] - cost[rows, 128 * t : 128 * (t + 1)] for t in range(cost.shape[1] // 128)]
    top = tree(jnp.maximum, values)
    tops[rows, :] = top
    sums[rows, :] = tree(jnp.add, [jnp.exp2(v - top) for v in values])


def row_finish(at, tops, sums):
    top = tops[at : at + 128, :].T
    highest = jnp.max(top, axis=0, keepdims=True)
    total = jnp.sum(sums[at : at + 128, :].T * jnp.exp2(top - highest), axis=0, keepdims=True)
    return highest + LOG2E * jnp.log(total)


CHUNK = 128
STRIP = 256


def col_strip(n, first, size, pot, cost, tops, sums, out):
    lanes = pl.ds(pl.multiple_of(n * STRIP, STRIP), STRIP)

    def chunk(k, carry):
        top, summed = carry
        rows = pl.ds(pl.multiple_of(first + k * CHUNK, CHUNK), CHUNK)
        p = pot[rows, :]
        values = jnp.concatenate([p] * (STRIP // 128), axis=1) - cost[rows, lanes]
        values = values.reshape(CHUNK // 8, 8, STRIP)
        now = jnp.maximum(top, jnp.max(values, axis=0))
        summed = summed * jnp.exp2(top - now) + jnp.sum(jnp.exp2(values - now[None]), axis=0)
        return now, summed

    if first == 0:
        start = (jnp.full((8, STRIP), LOW, F32), jnp.zeros((8, STRIP), F32))
    else:
        start = (tops[:, lanes], sums[:, lanes])
    top, summed = lax.fori_loop(0, size // CHUNK, chunk, start, unroll=4)
    if out is None:
        tops[:, lanes] = top
        sums[:, lanes] = summed
        return
    highest = jnp.max(top, axis=0, keepdims=True)
    total = jnp.sum(summed * jnp.exp2(top - highest), axis=0, keepdims=True)
    result = highest + LOG2E * jnp.log(total)
    for t in range(STRIP // 128):
        out[pl.ds(n * (STRIP // 128) + t, 1), :] = result[:, 128 * t : 128 * (t + 1)]


def combine(buffer):
    n = buffer.shape[0]
    top = buffer[0]
    for k in range(1, n):
        top = jnp.maximum(top, buffer[k])
    total = jnp.exp2(buffer[0] - top)
    for k in range(1, n):
        total = total + jnp.exp2(buffer[k] - top)
    return top + LOG2E * jnp.log(total)


def kernel(
    n_row, n_col, src_ref, tgt_ref, coupling_ref, prior_ref, f_ref, g_ref,
    weights, src_full, tgt_blocks, tgt_full, xs, xt, ys, us, terms,
    parts, gathered, middle, core, cost, pot, pot_tgt, tops, sums, row_tops, row_sums, by_col, by_pair, by_chip,
    send, recv,
):
    row, col = lax.axis_index("row"), lax.axis_index("col")
    core_id = lax.rem(row, 2)
    chip = row // 2
    n_chip = n_row // 2
    depth = lax.rem(chip, 4)
    y = chip // 4
    n_y = n_chip // 4
    sib = row + 1 - 2 * core_id
    rows_here, cols_here = coupling_ref.shape
    total_src, total_tgt = rows_here * n_row, cols_here * n_col
    group = 2 * n_col
    slot = core_id * n_col + col

    x_size = n_col // 2
    x_at, plane_half = lax.rem(col, x_size), col // x_size
    half_col = (1 - plane_half) * x_size + x_at
    next_x, last_x = lax.rem(x_at + 1, x_size), lax.rem(x_at + x_size - 1, x_size)
    x_near = [(row, plane_half * x_size + next_x), (row, plane_half * x_size + last_x)]
    half_peer = (row, half_col)
    z_near = [((y * 4 + lax.rem(depth + d, 4)) * 2 + core_id, col) for d in (1, 3)]
    y_peers = [((lax.rem(y + d, n_y) * 4 + depth) * 2 + core_id, col) for d in range(1, n_y)]
    col_peers = [(row, lax.rem(col + d, n_col)) for d in range(1, n_col)]
    chip_peers = [(lax.rem(chip + d, n_chip) * 2 + core_id, col) for d in range(1, n_chip)]
    pair_peer = (sib, col)
    group_peers = col_peers + [(sib, lax.rem(col + d, n_col)) for d in range(n_col)]

    def put(source, target, index, peer):
        pltpu.make_async_remote_copy(
            src_ref=source, dst_ref=target, send_sem=send.at[index], recv_sem=recv.at[index],
            device_id=peer, device_id_type=MESH,
        ).start()

    def await_recv(ref, index):
        pltpu.make_async_copy(ref, ref, recv.at[index]).wait()

    def await_send(ref, index):
        pltpu.make_async_copy(ref, ref, send.at[index]).wait()

    barrier = pltpu.get_barrier_semaphore()
    greeted = x_near + y_peers + z_near + [half_peer, pair_peer]
    for peer in greeted:
        pl.semaphore_signal(barrier, inc=1, device_id=peer, device_id_type=MESH)
    features = src_ref.shape[0]
    mine = pl.ds(pl.multiple_of(col * features, features), features)
    copy_w = pltpu.make_async_copy(coupling_ref, weights, recv.at[LOCAL_W])
    copy_s = pltpu.make_async_copy(src_ref, src_full.at[mine], recv.at[LOCAL_S])
    copy_t = pltpu.make_async_copy(tgt_ref, tgt_blocks.at[core_id, y, 0], recv.at[LOCAL_T])
    copy_t.start()
    copy_s.start()
    copy_w.start()
    pl.semaphore_wait(barrier, len(greeted))

    plane = tgt_blocks.at[core_id, y]
    for d in range(2):
        put(tgt_ref, plane.at[2 - d], TGT_Z, z_near[d])
    half = rows_here // 2
    halves = [slice(0, half), slice(half, rows_here)]
    def block_at(c, h):
        return src_full.at[pl.ds(pl.multiple_of(c * features, features), features), halves[h]]

    def near(c, h, k, source=None):
        for d in range(2):
            put(source or block_at(c, h), block_at(c, h), NEAR + 4 * (1 - d) + 2 * k + h, x_near[d])

    def onward(h, k):
        d = 1 - h
        side = plane_half if k == 0 else 1 - plane_half
        block = block_at(side * x_size + (last_x if d else next_x), h)
        await_recv(block, NEAR + 4 * d + 2 * k + h)
        put(block, block, FAR + 2 * k + h, x_near[1 - d])

    def arrived(h):
        for k in range(2):
            await_recv(block_at(col, h), NEAR + 4 * h + 2 * k + h)
            await_recv(block_at(col, h), FAR + 2 * k + h)

    for h in range(2):
        own = src_ref.at[:, halves[h]]
        put(own, block_at(col, h), SRC_Z + h, half_peer)
        near(col, h, 0, own)
    copy_t.wait()
    await_recv(tgt_blocks.at[0, 0, 0:2], TGT_Z)
    put(plane.at[2], plane.at[3], TGT_Z2, z_near[0])
    for peer in y_peers:
        put(plane.at[0:3], plane.at[0:3], TGT_Y, peer)
    await_recv(block_at(col, 0), SRC_Z)
    near(half_col, 0, 1)
    onward(0, 0)
    await_recv(block_at(col, 1), SRC_Z + 1)
    near(half_col, 1, 1)
    onward(1, 0)
    await_recv(tgt_blocks.at[0, 0, 0], TGT_Z2)
    for peer in y_peers:
        put(plane.at[3], plane.at[3], TGT_Y2, peer)
    onward(0, 1)
    onward(1, 1)
    put(plane, plane, TGT_C, pair_peer)
    await_recv(tgt_blocks.at[0, 0 : n_y - 1, 0:3], TGT_Y)
    for e in range(1, n_y):
        block = tgt_blocks.at[core_id, lax.rem(y + e, n_y), 0:3]
        put(block, block, TGT_C, pair_peer)
    await_recv(tgt_blocks.at[0, 0 : n_y - 1, 3], TGT_Y2)
    for e in range(1, n_y):
        block = tgt_blocks.at[core_id, lax.rem(y + e, n_y), 3]
        put(block, block, TGT_C, pair_peer)
    arrived(0)
    arrived(1)
    copy_s.wait()
    copy_w.wait()

    source_right(src_full, xs, 0, rows_here)
    await_recv(tgt_blocks.at[0], TGT_C)
    for k in range(n_chip):
        away = lax.rem(k % 4 - depth + 4, 4)
        at = away + (away // 2) * (5 - 2 * away)
        tgt_full[8 * k : 8 * k + 8, :] = jnp.concatenate([tgt_blocks[0, k // 4, at], tgt_blocks[1, k // 4, at]], axis=0)
    feature_major(tgt_full, ys)

    mixed = lax.dot_general(
        weights[...], ys[256:512, :], (((1,), (1,)), ((), ())), preferred_element_type=F32
    )
    terms[:, 0:256], terms[:, 256:512] = split(mixed)
    part = jnp.dot(xs[...], terms[...], preferred_element_type=F32)
    part = part[:, 0:256] + part[:, 256:512]
    at8 = lax.broadcasted_iota(jnp.int32, (8, 128), 0)
    lane8 = lax.broadcasted_iota(jnp.int32, (8, 128), 1)
    edge = jnp.where(at8 < 2, part[128:136, 0:128], 0.0)
    corner = part[128:136, 128:256]
    corner = jnp.concatenate([corner[6:8], corner[0:6]], axis=0)
    edge = jnp.where((at8 >= 2) & (at8 < 4), corner, edge)
    side = jnp.where(at8 < 2, part[0:128, 128:256].T[0:8], 0.0)
    for s in range(group):
        parts[s, 0:8, :] = part[8 * s : 8 * s + 8, 0:128]
        one = edge[s : s + 1] if s < 8 else side[s - 8 : s - 7]
        parts[s, 8:16, :] = jnp.where(at8 == 0, one, 0.0)

    def slot_of(peer):
        return lax.rem(peer[0], 2) * n_col + peer[1]

    for peer in group_peers:
        put(parts.at[slot_of(peer)], gathered.at[slot], SCATTER, peer)
    gathered[slot] = parts[slot]
    state_major(src_full, xt)
    await_recv(gathered.at[0 : group - 1], SCATTER)
    total = gathered[0]
    for k in range(1, group):
        total = total + gathered[k]
    middle[chip] = total
    for peer in chip_peers:
        put(middle.at[chip], middle.at[chip], MIDDLE, peer)
    pot_tgt[...] = prior_ref[...] * (LOG2E / EPSILON)
    await_recv(middle.at[0 : n_chip - 1], MIDDLE)
    total = middle[0]
    for k in range(1, n_chip):
        total = total + middle[k]
    core[slot] = total
    for peer in group_peers:
        put(core.at[slot], core.at[slot], SPREAD, peer)
    await_recv(core.at[0 : group - 1], SPREAD)

    scale = -2.0 * LOG2E / (EPSILON * total_src * total_tgt)
    main = jnp.concatenate([core[s, 0:8, :] for s in range(group)], axis=0) * (4.0 * scale)
    src_q, src_one = core[0, 8:9, :], core[1, 8:9, :]
    corner_q, corner_one = core[2, 8:9, :], core[3, 8:9, :]
    tgt_q, tgt_one = core[8, 8:9, :], core[9, 8:9, :]

    def pattern(at, first, second):
        value = jnp.where((at == 0) | (at == 2) | (at == 4), first, 0.0)
        return jnp.where((at == 1) | (at == 5), second, value)

    at16 = lax.broadcasted_iota(jnp.int32, (128, 128), 0)
    lane16 = lax.broadcasted_iota(jnp.int32, (128, 128), 1)
    lower_left = pattern(at16, src_one, src_q) * (-2.0 * scale)
    upper_right = pattern(at16, tgt_one, tgt_q).T * (-2.0 * scale)
    lower_right = pattern(
        at16,
        pattern(lane16, corner_one[:, 1:2], corner_one[:, 0:1]),
        pattern(lane16, corner_q[:, 1:2], corner_q[:, 0:1]),
    ) * scale
    left = jnp.concatenate([main, lower_left], axis=0)
    right = jnp.concatenate([upper_right, lower_right], axis=0)
    left_high, left_low = split(left)
    right_high, right_low = split(right)
    right_lane = lax.broadcasted_iota(jnp.int32, (256, 128), 1)
    ext = jnp.where(right_lane < 4, right_high.astype(F32), right_low.astype(F32)).astype(BF16)
    factor = jnp.concatenate([left_high, left_high, left_low, ext], axis=1)

    def factor_strip(n):
        cols = pl.ds(pl.multiple_of(n * 256, 256), 256)
        u = jnp.dot(factor, ys[:, cols], preferred_element_type=F32)
        high, low = split(u[0:128])
        us[0:128, cols] = high
        us[128:256, cols] = high
        us[256:384, cols] = low
        high, low = split(u[128:256])
        at = lax.broadcasted_iota(jnp.int32, (128, 256), 0)
        us[384:512, cols] = jnp.where(at < 4, high.astype(F32), low.astype(F32)).astype(BF16)

    n_strips = cols_here // 256

    def cost_strip(n, carry):
        lanes = pl.ds(pl.multiple_of(n * 256, 256), 256)
        cost[:, lanes] = jnp.dot(xt[...], us[:, lanes], preferred_element_type=F32)
        return carry

    def factor_loop(n, carry):
        factor_strip(n)
        return carry

    lax.fori_loop(0, n_strips, factor_loop, 0)
    lax.fori_loop(0, n_strips, cost_strip, 0)

    n_part = half // 128
    for sweep in range(SWEEPS):
        for h in range(2):
            mine_now = by_col.at[sweep, h, col]

            def block(b, carry):
                for q in range(8):
                    row_partial(h * half + b * 64 + 8 * q, pot_tgt, cost, row_tops, row_sums)
                return carry

            lax.fori_loop(0, half // 64, block, 0)
            for b in range(n_part):
                mine_now[b : b + 1, :] = row_finish(h * half + 128 * b, row_tops, row_sums)
            for peer in col_peers:
                put(mine_now, mine_now, ROWS + 2 * sweep + h, peer)
        f = []
        for h in range(2):
            await_recv(by_col.at[sweep, h, 0 : n_col - 1], ROWS + 2 * sweep + h)
            f.append(-math.log2(total_src) - combine(by_col.at[sweep, h]))
            down_rows(f[h], pot, h * half)
            out = by_pair.at[sweep, core_id] if h else None

            def strip(n, carry):
                col_strip(n, h * half, half, pot, cost, tops, sums, out)
                return carry

            lax.fori_loop(0, cols_here // STRIP, strip, 0)
        put(by_pair.at[sweep, core_id], by_pair.at[sweep, core_id], PAIR + sweep, pair_peer)
        await_recv(by_pair.at[sweep, 0], PAIR + sweep)
        by_chip[sweep, chip] = combine(by_pair.at[sweep])
        for peer in chip_peers:
            put(by_chip.at[sweep, chip], by_chip.at[sweep, chip], CHIPS + sweep, peer)
        await_recv(by_chip.at[sweep, 0 : n_chip - 1], CHIPS + sweep)
        g = -math.log2(total_tgt) - combine(by_chip.at[sweep])
        pot_tgt[...] = g
    f_ref[...] = jnp.concatenate(f, axis=0) * (EPSILON / LOG2E)
    g_ref[...] = g * (EPSILON / LOG2E)

    for h in range(2):
        await_send(block_at(col, h), SRC_Z + h)
        for k in range(2):
            await_send(block_at(col, h), FAR + 2 * k + h)
            for d in range(2):
                await_send(block_at(col, h), NEAR + 4 * d + 2 * k + h)
    await_send(tgt_blocks.at[0, 0, 0:2], TGT_Z)
    await_send(tgt_blocks.at[0, 0, 0], TGT_Z2)
    await_send(tgt_blocks.at[0, 0 : n_y - 1, 0:3], TGT_Y)
    await_send(tgt_blocks.at[0, 0 : n_y - 1, 3], TGT_Y2)
    await_send(tgt_blocks.at[0], TGT_C)
    await_send(gathered.at[0 : group - 1], SCATTER)
    await_send(middle.at[0 : n_chip - 1], MIDDLE)
    await_send(core.at[0 : group - 1], SPREAD)
    for sweep in range(SWEEPS):
        for h in range(2):
            await_send(by_col.at[sweep, h, 0 : n_col - 1], ROWS + 2 * sweep + h)
        await_send(by_pair.at[sweep, 0], PAIR + sweep)
        await_send(by_chip.at[sweep, 0 : n_chip - 1], CHIPS + sweep)


def solution(mesh):
    n_row, n_col = mesh.shape["row"], mesh.shape["col"]
    n_chip = n_row // 2
    group = 2 * n_col

    def local(src_pos, tgt_pos, coupling, prior_tgt):
        rows, cols = coupling.shape
        vmem = pl.BlockSpec(memory_space=pltpu.VMEM)
        anywhere = pl.BlockSpec(memory_space=pl.ANY)
        f, g = pl.pallas_call(
            lambda *refs: kernel(n_row, n_col, *refs),
            out_shape=[
                jax.ShapeDtypeStruct((rows // 128, 128), F32),
                jax.ShapeDtypeStruct((cols // 128, 128), F32),
            ],
            in_specs=[anywhere, anywhere, anywhere, vmem],
            out_specs=[vmem, vmem],
            scratch_shapes=[
                pltpu.VMEM((rows, cols), BF16),
                pltpu.VMEM((128, rows), F32),
                pltpu.VMEM((2, n_chip // 4, 4, 4, cols), F32),
                pltpu.VMEM((128, cols), F32),
                pltpu.VMEM((144, rows), BF16),
                pltpu.VMEM((rows, 512), BF16),
                pltpu.VMEM((512, cols), BF16),
                pltpu.VMEM((512, cols), BF16),
                pltpu.VMEM((rows, 512), BF16),
                pltpu.VMEM((group, 16, 128), F32),
                pltpu.VMEM((group, 16, 128), F32),
                pltpu.VMEM((n_chip, 16, 128), F32),
                pltpu.VMEM((group, 16, 128), F32),
                pltpu.VMEM((rows, cols), F32),
                pltpu.VMEM((rows, 128), F32),
                pltpu.VMEM((cols // 128, 128), F32),
                pltpu.VMEM((8, cols), F32),
                pltpu.VMEM((8, cols), F32),
                pltpu.VMEM((rows, 128), F32),
                pltpu.VMEM((rows, 128), F32),
                pltpu.VMEM((SWEEPS, 2, n_col, rows // 256, 128), F32),
                pltpu.VMEM((SWEEPS, 2, cols // 128, 128), F32),
                pltpu.VMEM((SWEEPS, n_chip, cols // 128, 128), F32),
                pltpu.SemaphoreType.DMA((SLOTS,)),
                pltpu.SemaphoreType.DMA((SLOTS,)),
            ],
            compiler_params=pltpu.CompilerParams(
                collective_id=0, has_side_effects=True, vmem_limit_bytes=63 * 2**20
            ),
        )(src_pos, tgt_pos, coupling, prior_tgt.reshape(cols // 128, 128))
        return f.reshape(rows), g.reshape(cols)

    placed = (P("col", "row"), P("row", "col"), P("row", "col"), P("col"))
    return jax.shard_map(
        local, mesh=mesh, in_specs=placed, out_specs=(P("row"), P("col")), check_vma=False
    )
```

```python
import math

import jax
import jax.numpy as jnp
from jax import lax
from jax.experimental import pallas as pl
from jax.experimental.pallas import tpu as pltpu
from jax.sharding import PartitionSpec as P

SWEEPS = 2
EPSILON = 0.25
LOG2E = 1.4426950408889634
MESH = pl.DeviceIdType.MESH
F32 = jnp.float32
BF16 = jnp.bfloat16
LOW = -3.0e38

TGT_Z, TGT_Z2, TGT_Y, TGT_Y2, TGT_C, SCATTER, MIDDLE, SPREAD, LOCAL_W, LOCAL_S, LOCAL_T = range(11)
SRC_Z, ROWS, PAIR, CHIPS, NEAR, FAR = 11, 13, 17, 21, 25, 33
SLOTS = 37


def split(value):
    high = value.astype(BF16)
    return high, (value - high.astype(F32)).astype(BF16)


def extension(x, shape, axis):
    q = jnp.sum(x * x, axis=axis, keepdims=True)
    q_high = q.astype(BF16).astype(F32)
    at = lax.broadcasted_iota(jnp.int32, shape, axis)
    ext = jnp.where((at == 1) | (at == 5), 1.0, 0.0)
    ext = jnp.where((at == 0) | (at == 4), q_high, ext)
    return jnp.where(at == 2, q - q_high, ext).astype(BF16)


def source_right(x_ref, stack, first, size):
    def block(b, carry):
        cols = pl.ds(pl.multiple_of(first + b * 512, 512), 512)
        x = x_ref[:, cols]
        stack[0:128, cols] = x.astype(BF16)
        stack[128:144, cols] = extension(x, (16, 512), 0)
        return carry

    lax.fori_loop(0, size // 512, block, 0)


def feature_major(x_ref, stack):
    def block(b, carry):
        cols = pl.ds(pl.multiple_of(b * 512, 512), 512)
        x = x_ref[:, cols]
        high, low = split(x)
        stack[0:128, cols] = high
        stack[128:256, cols] = low
        stack[256:384, cols] = high
        stack[384:400, cols] = extension(x, (16, 512), 0)
        stack[400:512, cols] = jnp.zeros((112, 512), BF16)
        return carry

    lax.fori_loop(0, x_ref.shape[1] // 512, block, 0)


def state_major(x_ref, stack):
    size = x_ref.shape[1]

    def block(b, carry):
        at = pl.ds(pl.multiple_of(b * 128, 128), 128)
        x = x_ref[:, at].T
        high, low = split(x)
        stack[at, 0:128] = high
        stack[at, 128:256] = low
        stack[at, 256:384] = high
        stack[at, 384:512] = extension(x, (128, 128), 1)
        return carry

    lax.fori_loop(0, size // 128, block, 0)


def down_rows(vector, out, first):
    for b in range(vector.shape[0]):
        at = first + 128 * b
        out[at : at + 128, :] = jnp.broadcast_to(vector[b : b + 1, :], (128, 128)).T


def tree(op, terms):
    while len(terms) > 1:
        terms = [op(*terms[k : k + 2]) if k + 1 < len(terms) else terms[k] for k in range(0, len(terms), 2)]
    return terms[0]


def row_partial(at, pot, cost, tops, sums):
    rows = pl.ds(pl.multiple_of(at, 8), 8)
    values = [pot[t : t + 1, :] - cost[rows, 128 * t : 128 * (t + 1)] for t in range(cost.shape[1] // 128)]
    top = tree(jnp.maximum, values)
    tops[rows, :] = top
    sums[rows, :] = tree(jnp.add, [jnp.exp2(v - top) for v in values])


def row_finish(at, tops, sums):
    top = tops[at : at + 128, :].T
    highest = jnp.max(top, axis=0, keepdims=True)
    total = jnp.sum(sums[at : at + 128, :].T * jnp.exp2(top - highest), axis=0, keepdims=True)
    return highest + LOG2E * jnp.log(total)


CHUNK = 128
STRIP = 256


def col_strip(n, lane, first, size, pot, cost, tops, sums, out):
    lanes = pl.ds(pl.multiple_of(lane + n * STRIP, STRIP), STRIP)

    def chunk(k, carry):
        top, summed = carry
        rows = pl.ds(pl.multiple_of(first + k * CHUNK, CHUNK), CHUNK)
        p = pot[rows, :]
        values = jnp.concatenate([p] * (STRIP // 128), axis=1) - cost[rows, lanes]
        values = values.reshape(CHUNK // 8, 8, STRIP)
        now = jnp.maximum(top, jnp.max(values, axis=0))
        summed = summed * jnp.exp2(top - now) + jnp.sum(jnp.exp2(values - now[None]), axis=0)
        return now, summed

    if first == 0:
        start = (jnp.full((8, STRIP), LOW, F32), jnp.zeros((8, STRIP), F32))
    else:
        start = (tops[:, lanes], sums[:, lanes])
    top, summed = lax.fori_loop(0, size // CHUNK, chunk, start, unroll=4)
    if out is None:
        tops[:, lanes] = top
        sums[:, lanes] = summed
        return
    highest = jnp.max(top, axis=0, keepdims=True)
    total = jnp.sum(summed * jnp.exp2(top - highest), axis=0, keepdims=True)
    result = highest + LOG2E * jnp.log(total)
    for t in range(STRIP // 128):
        out[pl.ds(n * (STRIP // 128) + t, 1), :] = result[:, 128 * t : 128 * (t + 1)]


def combine(buffer):
    n = buffer.shape[0]
    top = buffer[0]
    for k in range(1, n):
        top = jnp.maximum(top, buffer[k])
    total = jnp.exp2(buffer[0] - top)
    for k in range(1, n):
        total = total + jnp.exp2(buffer[k] - top)
    return top + LOG2E * jnp.log(total)


def kernel(
    n_row, n_col, src_ref, tgt_ref, coupling_ref, prior_ref, f_ref, g_ref,
    weights, src_full, tgt_blocks, tgt_full, xs, xt, ys, us, terms,
    parts, gathered, middle, core, cost, pot, pot_tgt, tops, sums, row_tops, row_sums, by_col, by_pair, by_chip,
    send, recv,
):
    row, col = lax.axis_index("row"), lax.axis_index("col")
    core_id = lax.rem(row, 2)
    chip = row // 2
    n_chip = n_row // 2
    depth = lax.rem(chip, 4)
    y = chip // 4
    n_y = n_chip // 4
    sib = row + 1 - 2 * core_id
    rows_here, cols_here = coupling_ref.shape
    total_src, total_tgt = rows_here * n_row, cols_here * n_col
    group = 2 * n_col
    slot = core_id * n_col + col

    x_size = n_col // 2
    x_at, plane_half = lax.rem(col, x_size), col // x_size
    half_col = (1 - plane_half) * x_size + x_at
    next_x, last_x = lax.rem(x_at + 1, x_size), lax.rem(x_at + x_size - 1, x_size)
    x_near = [(row, plane_half * x_size + next_x), (row, plane_half * x_size + last_x)]
    half_peer = (row, half_col)
    z_near = [((y * 4 + lax.rem(depth + d, 4)) * 2 + core_id, col) for d in (1, 3)]
    y_peers = [((lax.rem(y + d, n_y) * 4 + depth) * 2 + core_id, col) for d in range(1, n_y)]
    col_peers = [(row, lax.rem(col + d, n_col)) for d in range(1, n_col)]
    chip_peers = [(lax.rem(chip + d, n_chip) * 2 + core_id, col) for d in range(1, n_chip)]
    pair_peer = (sib, col)
    group_peers = col_peers + [(sib, lax.rem(col + d, n_col)) for d in range(n_col)]

    def put(source, target, index, peer):
        pltpu.make_async_remote_copy(
            src_ref=source, dst_ref=target, send_sem=send.at[index], recv_sem=recv.at[index],
            device_id=peer, device_id_type=MESH,
        ).start()

    def await_recv(ref, index):
        pltpu.make_async_copy(ref, ref, recv.at[index]).wait()

    def await_send(ref, index):
        pltpu.make_async_copy(ref, ref, send.at[index]).wait()

    barrier = pltpu.get_barrier_semaphore()
    greeted = x_near + y_peers + z_near + [half_peer, pair_peer]
    for peer in greeted:
        pl.semaphore_signal(barrier, inc=1, device_id=peer, device_id_type=MESH)
    features = src_ref.shape[0]
    mine = pl.ds(pl.multiple_of(col * features, features), features)
    copy_w = pltpu.make_async_copy(coupling_ref, weights, recv.at[LOCAL_W])
    copy_s = pltpu.make_async_copy(src_ref, src_full.at[mine], recv.at[LOCAL_S])
    copy_t = pltpu.make_async_copy(tgt_ref, tgt_blocks.at[core_id, y, 0], recv.at[LOCAL_T])
    copy_t.start()
    copy_s.start()
    copy_w.start()
    pl.semaphore_wait(barrier, len(greeted))

    plane = tgt_blocks.at[core_id, y]
    for d in range(2):
        put(tgt_ref, plane.at[2 - d], TGT_Z, z_near[d])
    half = rows_here // 2
    halves = [slice(0, half), slice(half, rows_here)]
    def block_at(c, h):
        return src_full.at[pl.ds(pl.multiple_of(c * features, features), features), halves[h]]

    def near(c, h, k, source=None):
        for d in range(2):
            put(source or block_at(c, h), block_at(c, h), NEAR + 4 * (1 - d) + 2 * k + h, x_near[d])

    def onward(h, k):
        d = 1 - h
        side = plane_half if k == 0 else 1 - plane_half
        block = block_at(side * x_size + (last_x if d else next_x), h)
        await_recv(block, NEAR + 4 * d + 2 * k + h)
        put(block, block, FAR + 2 * k + h, x_near[1 - d])

    def arrived(h):
        for k in range(2):
            await_recv(block_at(col, h), NEAR + 4 * h + 2 * k + h)
            await_recv(block_at(col, h), FAR + 2 * k + h)

    for h in range(2):
        own = src_ref.at[:, halves[h]]
        put(own, block_at(col, h), SRC_Z + h, half_peer)
        near(col, h, 0, own)
    copy_t.wait()
    await_recv(tgt_blocks.at[0, 0, 0:2], TGT_Z)
    put(plane.at[2], plane.at[3], TGT_Z2, z_near[0])
    for peer in y_peers:
        put(plane.at[0:3], plane.at[0:3], TGT_Y, peer)
    await_recv(block_at(col, 0), SRC_Z)
    near(half_col, 0, 1)
    onward(0, 0)
    await_recv(block_at(col, 1), SRC_Z + 1)
    near(half_col, 1, 1)
    onward(1, 0)
    await_recv(tgt_blocks.at[0, 0, 0], TGT_Z2)
    for peer in y_peers:
        put(plane.at[3], plane.at[3], TGT_Y2, peer)
    onward(0, 1)
    onward(1, 1)
    put(plane, plane, TGT_C, pair_peer)
    await_recv(tgt_blocks.at[0, 0 : n_y - 1, 0:3], TGT_Y)
    for e in range(1, n_y):
        block = tgt_blocks.at[core_id, lax.rem(y + e, n_y), 0:3]
        put(block, block, TGT_C, pair_peer)
    await_recv(tgt_blocks.at[0, 0 : n_y - 1, 3], TGT_Y2)
    for e in range(1, n_y):
        block = tgt_blocks.at[core_id, lax.rem(y + e, n_y), 3]
        put(block, block, TGT_C, pair_peer)
    arrived(0)
    arrived(1)
    copy_s.wait()
    copy_w.wait()

    source_right(src_full, xs, 0, rows_here)
    await_recv(tgt_blocks.at[0], TGT_C)
    for k in range(n_chip):
        away = lax.rem(k % 4 - depth + 4, 4)
        at = away + (away // 2) * (5 - 2 * away)
        tgt_full[8 * k : 8 * k + 8, :] = jnp.concatenate([tgt_blocks[0, k // 4, at], tgt_blocks[1, k // 4, at]], axis=0)
    feature_major(tgt_full, ys)

    mixed = lax.dot_general(
        weights[...], ys[256:512, :], (((1,), (1,)), ((), ())), preferred_element_type=F32
    )
    terms[:, 0:256], terms[:, 256:512] = split(mixed)
    part = jnp.dot(xs[...], terms[...], preferred_element_type=F32)
    part = part[:, 0:256] + part[:, 256:512]
    at8 = lax.broadcasted_iota(jnp.int32, (8, 128), 0)
    lane8 = lax.broadcasted_iota(jnp.int32, (8, 128), 1)
    edge = jnp.where(at8 < 2, part[128:136, 0:128], 0.0)
    corner = part[128:136, 128:256]
    corner = jnp.concatenate([corner[6:8], corner[0:6]], axis=0)
    edge = jnp.where((at8 >= 2) & (at8 < 4), corner, edge)
    side = jnp.where(at8 < 2, part[0:128, 128:256].T[0:8], 0.0)
    for s in range(group):
        parts[s, 0:8, :] = part[8 * s : 8 * s + 8, 0:128]
        one = edge[s : s + 1] if s < 8 else side[s - 8 : s - 7]
        parts[s, 8:16, :] = jnp.where(at8 == 0, one, 0.0)

    def slot_of(peer):
        return lax.rem(peer[0], 2) * n_col + peer[1]

    for peer in group_peers:
        put(parts.at[slot_of(peer)], gathered.at[slot], SCATTER, peer)
    gathered[slot] = parts[slot]
    state_major(src_full, xt)
    await_recv(gathered.at[0 : group - 1], SCATTER)
    total = gathered[0]
    for k in range(1, group):
        total = total + gathered[k]
    middle[chip] = total
    for peer in chip_peers:
        put(middle.at[chip], middle.at[chip], MIDDLE, peer)
    pot_tgt[...] = prior_ref[...] * (LOG2E / EPSILON)
    await_recv(middle.at[0 : n_chip - 1], MIDDLE)
    total = middle[0]
    for k in range(1, n_chip):
        total = total + middle[k]
    core[slot] = total
    for peer in group_peers:
        put(core.at[slot], core.at[slot], SPREAD, peer)
    await_recv(core.at[0 : group - 1], SPREAD)

    scale = -2.0 * LOG2E / (EPSILON * total_src * total_tgt)
    main = jnp.concatenate([core[s, 0:8, :] for s in range(group)], axis=0) * (4.0 * scale)
    src_q, src_one = core[0, 8:9, :], core[1, 8:9, :]
    corner_q, corner_one = core[2, 8:9, :], core[3, 8:9, :]
    tgt_q, tgt_one = core[8, 8:9, :], core[9, 8:9, :]

    def pattern(at, first, second):
        value = jnp.where((at == 0) | (at == 2) | (at == 4), first, 0.0)
        return jnp.where((at == 1) | (at == 5), second, value)

    at16 = lax.broadcasted_iota(jnp.int32, (128, 128), 0)
    lane16 = lax.broadcasted_iota(jnp.int32, (128, 128), 1)
    lower_left = pattern(at16, src_one, src_q) * (-2.0 * scale)
    upper_right = pattern(at16, tgt_one, tgt_q).T * (-2.0 * scale)
    lower_right = pattern(
        at16,
        pattern(lane16, corner_one[:, 1:2], corner_one[:, 0:1]),
        pattern(lane16, corner_q[:, 1:2], corner_q[:, 0:1]),
    ) * scale
    left = jnp.concatenate([main, lower_left], axis=0)
    right = jnp.concatenate([upper_right, lower_right], axis=0)
    left_high, left_low = split(left)
    right_high, right_low = split(right)
    right_lane = lax.broadcasted_iota(jnp.int32, (256, 128), 1)
    ext = jnp.where(right_lane < 4, right_high.astype(F32), right_low.astype(F32)).astype(BF16)
    factor = jnp.concatenate([left_high, left_high, left_low, ext], axis=1)

    def factor_strip(n):
        cols = pl.ds(pl.multiple_of(n * 256, 256), 256)
        u = jnp.dot(factor, ys[:, cols], preferred_element_type=F32)
        high, low = split(u[0:128])
        us[0:128, cols] = high
        us[128:256, cols] = high
        us[256:384, cols] = low
        high, low = split(u[128:256])
        at = lax.broadcasted_iota(jnp.int32, (128, 256), 0)
        us[384:512, cols] = jnp.where(at < 4, high.astype(F32), low.astype(F32)).astype(BF16)

    n_strips = cols_here // 256

    def cost_of(n):
        lanes = pl.ds(pl.multiple_of(n * 256, 256), 256)
        cost[:, lanes] = jnp.dot(xt[...], us[:, lanes], preferred_element_type=F32)

    def cost_strip(n, carry):
        cost_of(n)
        factor_strip(n + 1)
        return carry

    factor_strip(0)
    lax.fori_loop(0, n_strips - 1, cost_strip, 0)
    cost_of(n_strips - 1)

    n_part = half // 128
    n_lanes = cols_here // 2
    for sweep in range(SWEEPS):
        for h in range(2):
            mine_now = by_col.at[sweep, h, col]

            def block(b, carry):
                for q in range(8):
                    row_partial(h * half + b * 64 + 8 * q, pot_tgt, cost, row_tops, row_sums)
                return carry

            lax.fori_loop(0, half // 64, block, 0)
            for b in range(n_part):
                mine_now[b : b + 1, :] = row_finish(h * half + 128 * b, row_tops, row_sums)
            for peer in col_peers:
                put(mine_now, mine_now, ROWS + 2 * sweep + h, peer)
        f = []
        for h in range(2):
            await_recv(by_col.at[sweep, h, 0 : n_col - 1], ROWS + 2 * sweep + h)
            f.append(-math.log2(total_src) - combine(by_col.at[sweep, h]))
            down_rows(f[h], pot, h * half)

            for j in range(2):
                out = by_pair.at[sweep, j, core_id] if h else None

                def strip(n, carry):
                    col_strip(n, j * n_lanes, h * half, half, pot, cost, tops, sums, out)
                    return carry

                lax.fori_loop(0, n_lanes // STRIP, strip, 0)
                if h:
                    put(out, out, PAIR + 2 * sweep + j, pair_peer)
        for j in range(2):
            await_recv(by_pair.at[sweep, j, 0], PAIR + 2 * sweep + j)
            mine_now = by_chip.at[sweep, j, chip]
            mine_now[...] = combine(by_pair.at[sweep, j])
            for peer in chip_peers:
                put(mine_now, mine_now, CHIPS + 2 * sweep + j, peer)
        g = []
        for j in range(2):
            await_recv(by_chip.at[sweep, j, 0 : n_chip - 1], CHIPS + 2 * sweep + j)
            g.append(-math.log2(total_tgt) - combine(by_chip.at[sweep, j]))
        pot_tgt[...] = jnp.concatenate(g, axis=0)
    f_ref[...] = jnp.concatenate(f, axis=0) * (EPSILON / LOG2E)
    g_ref[...] = jnp.concatenate(g, axis=0) * (EPSILON / LOG2E)

    for h in range(2):
        await_send(block_at(col, h), SRC_Z + h)
        for k in range(2):
            await_send(block_at(col, h), FAR + 2 * k + h)
            for d in range(2):
                await_send(block_at(col, h), NEAR + 4 * d + 2 * k + h)
    await_send(tgt_blocks.at[0, 0, 0:2], TGT_Z)
    await_send(tgt_blocks.at[0, 0, 0], TGT_Z2)
    await_send(tgt_blocks.at[0, 0 : n_y - 1, 0:3], TGT_Y)
    await_send(tgt_blocks.at[0, 0 : n_y - 1, 3], TGT_Y2)
    await_send(tgt_blocks.at[0], TGT_C)
    await_send(gathered.at[0 : group - 1], SCATTER)
    await_send(middle.at[0 : n_chip - 1], MIDDLE)
    await_send(core.at[0 : group - 1], SPREAD)
    for sweep in range(SWEEPS):
        for h in range(2):
            await_send(by_col.at[sweep, h, 0 : n_col - 1], ROWS + 2 * sweep + h)
        for j in range(2):
            await_send(by_pair.at[sweep, j, 0], PAIR + 2 * sweep + j)
            await_send(by_chip.at[sweep, j, 0 : n_chip - 1], CHIPS + 2 * sweep + j)


def solution(mesh):
    n_row, n_col = mesh.shape["row"], mesh.shape["col"]
    n_chip = n_row // 2
    group = 2 * n_col

    def local(src_pos, tgt_pos, coupling, prior_tgt):
        rows, cols = coupling.shape
        vmem = pl.BlockSpec(memory_space=pltpu.VMEM)
        anywhere = pl.BlockSpec(memory_space=pl.ANY)
        f, g = pl.pallas_call(
            lambda *refs: kernel(n_row, n_col, *refs),
            out_shape=[
                jax.ShapeDtypeStruct((rows // 128, 128), F32),
                jax.ShapeDtypeStruct((cols // 128, 128), F32),
            ],
            in_specs=[anywhere, anywhere, anywhere, vmem],
            out_specs=[vmem, vmem],
            scratch_shapes=[
                pltpu.VMEM((rows, cols), BF16),
                pltpu.VMEM((128, rows), F32),
                pltpu.VMEM((2, n_chip // 4, 4, 4, cols), F32),
                pltpu.VMEM((128, cols), F32),
                pltpu.VMEM((144, rows), BF16),
                pltpu.VMEM((rows, 512), BF16),
                pltpu.VMEM((512, cols), BF16),
                pltpu.VMEM((512, cols), BF16),
                pltpu.VMEM((rows, 512), BF16),
                pltpu.VMEM((group, 16, 128), F32),
                pltpu.VMEM((group, 16, 128), F32),
                pltpu.VMEM((n_chip, 16, 128), F32),
                pltpu.VMEM((group, 16, 128), F32),
                pltpu.VMEM((rows, cols), F32),
                pltpu.VMEM((rows, 128), F32),
                pltpu.VMEM((cols // 128, 128), F32),
                pltpu.VMEM((8, cols), F32),
                pltpu.VMEM((8, cols), F32),
                pltpu.VMEM((rows, 128), F32),
                pltpu.VMEM((rows, 128), F32),
                pltpu.VMEM((SWEEPS, 2, n_col, rows // 256, 128), F32),
                pltpu.VMEM((SWEEPS, 2, 2, cols // 256, 128), F32),
                pltpu.VMEM((SWEEPS, 2, n_chip, cols // 256, 128), F32),
                pltpu.SemaphoreType.DMA((SLOTS,)),
                pltpu.SemaphoreType.DMA((SLOTS,)),
            ],
            compiler_params=pltpu.CompilerParams(
                collective_id=0, has_side_effects=True, vmem_limit_bytes=63 * 2**20
            ),
        )(src_pos, tgt_pos, coupling, prior_tgt.reshape(cols // 128, 128))
        return f.reshape(rows), g.reshape(cols)

    placed = (P("col", "row"), P("row", "col"), P("row", "col"), P("col"))
    return jax.shard_map(
        local, mesh=mesh, in_specs=placed, out_specs=(P("row"), P("col")), check_vma=False
    )
```

```python
import math

import jax
import jax.numpy as jnp
from jax import lax
from jax.experimental import pallas as pl
from jax.experimental.pallas import tpu as pltpu
from jax.sharding import PartitionSpec as P

SWEEPS = 2
EPSILON = 0.25
LOG2E = 1.4426950408889634
MESH = pl.DeviceIdType.MESH
F32 = jnp.float32
BF16 = jnp.bfloat16
LOW = -3.0e38

TGT_Z, TGT_Z2, TGT_Y, TGT_Y2, TGT_C, SCATTER, MIDDLE, SPREAD, LOCAL_W, LOCAL_S, LOCAL_T = range(11)
SRC_Z, ROWS, PAIR, CHIPS, NEAR, FAR = 11, 13, 17, 21, 25, 33
SLOTS = 37


def split(value):
    high = value.astype(BF16)
    return high, (value - high.astype(F32)).astype(BF16)


def extension(x, shape, axis):
    q = jnp.sum(x * x, axis=axis, keepdims=True)
    q_high = q.astype(BF16).astype(F32)
    at = lax.broadcasted_iota(jnp.int32, shape, axis)
    ext = jnp.where((at == 1) | (at == 5), 1.0, 0.0)
    ext = jnp.where((at == 0) | (at == 4), q_high, ext)
    return jnp.where(at == 2, q - q_high, ext).astype(BF16)


def source_right(x_ref, stack, first, size):
    def block(b, carry):
        cols = pl.ds(pl.multiple_of(first + b * 512, 512), 512)
        x = x_ref[:, cols]
        stack[0:128, cols] = x.astype(BF16)
        stack[128:144, cols] = extension(x, (16, 512), 0)
        return carry

    lax.fori_loop(0, size // 512, block, 0)


def feature_major(x_ref, stack):
    def block(b, carry):
        cols = pl.ds(pl.multiple_of(b * 512, 512), 512)
        x = x_ref[:, cols]
        high, low = split(x)
        stack[0:128, cols] = high
        stack[128:256, cols] = low
        stack[256:384, cols] = high
        stack[384:400, cols] = extension(x, (16, 512), 0)
        stack[400:512, cols] = jnp.zeros((112, 512), BF16)
        return carry

    lax.fori_loop(0, x_ref.shape[1] // 512, block, 0)


def state_major(x_ref, stack):
    size = x_ref.shape[1]

    def block(b, carry):
        at = pl.ds(pl.multiple_of(b * 128, 128), 128)
        x = x_ref[:, at].T
        high, low = split(x)
        stack[at, 0:128] = high
        stack[at, 128:256] = low
        stack[at, 256:384] = high
        stack[at, 384:512] = extension(x, (128, 128), 1)
        return carry

    lax.fori_loop(0, size // 128, block, 0)


def down_rows(vector, out, first):
    for b in range(vector.shape[0]):
        at = first + 128 * b
        out[at : at + 128, :] = jnp.broadcast_to(vector[b : b + 1, :], (128, 128)).T


def tree(op, terms):
    while len(terms) > 1:
        terms = [op(*terms[k : k + 2]) if k + 1 < len(terms) else terms[k] for k in range(0, len(terms), 2)]
    return terms[0]


def row_partial(at, pot, cost, tops, sums):
    rows = pl.ds(pl.multiple_of(at, 8), 8)
    values = [pot[t : t + 1, :] - cost[rows, 128 * t : 128 * (t + 1)] for t in range(cost.shape[1] // 128)]
    top = tree(jnp.maximum, values)
    tops[rows, :] = top
    sums[rows, :] = tree(jnp.add, [jnp.exp2(v - top) for v in values])


def row_finish(at, tops, sums):
    top = tops[at : at + 128, :].T
    highest = jnp.max(top, axis=0, keepdims=True)
    total = jnp.sum(sums[at : at + 128, :].T * jnp.exp2(top - highest), axis=0, keepdims=True)
    return highest + LOG2E * jnp.log(total)


CHUNK = 128
STRIP = 256


def col_strip(n, lane, first, size, pot, cost, tops, sums, out):
    lanes = pl.ds(pl.multiple_of(lane + n * STRIP, STRIP), STRIP)

    def chunk(k, carry):
        top, summed = carry
        rows = pl.ds(pl.multiple_of(first + k * CHUNK, CHUNK), CHUNK)
        p = pot[rows, :]
        values = jnp.concatenate([p] * (STRIP // 128), axis=1) - cost[rows, lanes]
        values = values.reshape(CHUNK // 8, 8, STRIP)
        now = jnp.maximum(top, jnp.max(values, axis=0))
        summed = summed * jnp.exp2(top - now) + jnp.sum(jnp.exp2(values - now[None]), axis=0)
        return now, summed

    if first == 0:
        start = (jnp.full((8, STRIP), LOW, F32), jnp.zeros((8, STRIP), F32))
    else:
        start = (tops[:, lanes], sums[:, lanes])
    top, summed = lax.fori_loop(0, size // CHUNK, chunk, start, unroll=4)
    if out is None:
        tops[:, lanes] = top
        sums[:, lanes] = summed
        return
    highest = jnp.max(top, axis=0, keepdims=True)
    total = jnp.sum(summed * jnp.exp2(top - highest), axis=0, keepdims=True)
    result = highest + LOG2E * jnp.log(total)
    for t in range(STRIP // 128):
        out[pl.ds(n * (STRIP // 128) + t, 1), :] = result[:, 128 * t : 128 * (t + 1)]


def combine(buffer):
    n = buffer.shape[0]
    top = buffer[0]
    for k in range(1, n):
        top = jnp.maximum(top, buffer[k])
    total = jnp.exp2(buffer[0] - top)
    for k in range(1, n):
        total = total + jnp.exp2(buffer[k] - top)
    return top + LOG2E * jnp.log(total)


def kernel(
    n_row, n_col, src_ref, tgt_ref, coupling_ref, prior_ref, f_ref, g_ref,
    weights, src_full, tgt_blocks, tgt_full, xs, xt, ys, us, terms,
    parts, gathered, middle, core, cost, pot, pot_tgt, tops, sums, row_tops, row_sums, by_col, by_pair, by_chip,
    send, recv,
):
    row, col = lax.axis_index("row"), lax.axis_index("col")
    core_id = lax.rem(row, 2)
    chip = row // 2
    n_chip = n_row // 2
    depth = lax.rem(chip, 4)
    y = chip // 4
    n_y = n_chip // 4
    sib = row + 1 - 2 * core_id
    rows_here, cols_here = coupling_ref.shape
    total_src, total_tgt = rows_here * n_row, cols_here * n_col
    group = 2 * n_col
    slot = core_id * n_col + col

    x_size = n_col // 2
    x_at, plane_half = lax.rem(col, x_size), col // x_size
    half_col = (1 - plane_half) * x_size + x_at
    next_x, last_x = lax.rem(x_at + 1, x_size), lax.rem(x_at + x_size - 1, x_size)
    x_near = [(row, plane_half * x_size + next_x), (row, plane_half * x_size + last_x)]
    half_peer = (row, half_col)
    z_near = [((y * 4 + lax.rem(depth + d, 4)) * 2 + core_id, col) for d in (1, 3)]
    y_peers = [((lax.rem(y + d, n_y) * 4 + depth) * 2 + core_id, col) for d in range(1, n_y)]
    steps = sorted(
        ((dx, dh) for dx in range(x_size) for dh in range(2)),
        key=lambda d: -min(d[0], x_size - d[0]) - d[1],
    )
    sides = (plane_half, 1 - plane_half)
    cols_by_hops = [sides[dh] * x_size + lax.rem(x_at + dx, x_size) for dx, dh in steps]
    col_peers = [(row, c) for c in cols_by_hops[:-1]]
    group_peers = [(r, c) for c in cols_by_hops[:-1] for r in (row, sib)] + [(sib, col)]
    chip_steps = sorted(
        ((dy, dz) for dy in range(n_y) for dz in range(4)),
        key=lambda d: -min(d[0], n_y - d[0]) - 2 * min(d[1], 4 - d[1]),
    )
    chip_peers = [
        ((lax.rem(y + dy, n_y) * 4 + lax.rem(depth + dz, 4)) * 2 + core_id, col)
        for dy, dz in chip_steps[:-1]
    ]
    pair_peer = (sib, col)

    def put(source, target, index, peer):
        pltpu.make_async_remote_copy(
            src_ref=source, dst_ref=target, send_sem=send.at[index], recv_sem=recv.at[index],
            device_id=peer, device_id_type=MESH,
        ).start()

    def await_recv(ref, index):
        pltpu.make_async_copy(ref, ref, recv.at[index]).wait()

    def await_send(ref, index):
        pltpu.make_async_copy(ref, ref, send.at[index]).wait()

    barrier = pltpu.get_barrier_semaphore()
    greeted = x_near + y_peers + z_near + [half_peer, pair_peer]
    for peer in greeted:
        pl.semaphore_signal(barrier, inc=1, device_id=peer, device_id_type=MESH)
    features = src_ref.shape[0]
    mine = pl.ds(pl.multiple_of(col * features, features), features)
    copy_w = pltpu.make_async_copy(coupling_ref, weights, recv.at[LOCAL_W])
    copy_s = pltpu.make_async_copy(src_ref, src_full.at[mine], recv.at[LOCAL_S])
    copy_t = pltpu.make_async_copy(tgt_ref, tgt_blocks.at[core_id, y, 0], recv.at[LOCAL_T])
    copy_t.start()
    copy_s.start()
    copy_w.start()
    pl.semaphore_wait(barrier, len(greeted))

    plane = tgt_blocks.at[core_id, y]
    for d in range(2):
        put(tgt_ref, plane.at[2 - d], TGT_Z, z_near[d])
    half = rows_here // 2
    halves = [slice(0, half), slice(half, rows_here)]
    def block_at(c, h):
        return src_full.at[pl.ds(pl.multiple_of(c * features, features), features), halves[h]]

    def near(c, h, k, source=None):
        for d in range(2):
            put(source or block_at(c, h), block_at(c, h), NEAR + 4 * (1 - d) + 2 * k + h, x_near[d])

    def onward(h, k):
        d = 1 - h
        side = plane_half if k == 0 else 1 - plane_half
        block = block_at(side * x_size + (last_x if d else next_x), h)
        await_recv(block, NEAR + 4 * d + 2 * k + h)
        put(block, block, FAR + 2 * k + h, x_near[1 - d])

    def arrived(h):
        for k in range(2):
            await_recv(block_at(col, h), NEAR + 4 * h + 2 * k + h)
            await_recv(block_at(col, h), FAR + 2 * k + h)

    for h in range(2):
        own = src_ref.at[:, halves[h]]
        put(own, block_at(col, h), SRC_Z + h, half_peer)
        near(col, h, 0, own)
    copy_t.wait()
    await_recv(tgt_blocks.at[0, 0, 0:2], TGT_Z)
    put(plane.at[2], plane.at[3], TGT_Z2, z_near[0])
    for peer in y_peers:
        put(plane.at[0:3], plane.at[0:3], TGT_Y, peer)
    await_recv(block_at(col, 0), SRC_Z)
    near(half_col, 0, 1)
    onward(0, 0)
    await_recv(block_at(col, 1), SRC_Z + 1)
    near(half_col, 1, 1)
    onward(1, 0)
    await_recv(tgt_blocks.at[0, 0, 0], TGT_Z2)
    for peer in y_peers:
        put(plane.at[3], plane.at[3], TGT_Y2, peer)
    onward(0, 1)
    onward(1, 1)
    put(plane, plane, TGT_C, pair_peer)
    await_recv(tgt_blocks.at[0, 0 : n_y - 1, 0:3], TGT_Y)
    for e in range(1, n_y):
        block = tgt_blocks.at[core_id, lax.rem(y + e, n_y), 0:3]
        put(block, block, TGT_C, pair_peer)
    await_recv(tgt_blocks.at[0, 0 : n_y - 1, 3], TGT_Y2)
    for e in range(1, n_y):
        block = tgt_blocks.at[core_id, lax.rem(y + e, n_y), 3]
        put(block, block, TGT_C, pair_peer)
    arrived(0)
    arrived(1)
    copy_s.wait()
    copy_w.wait()

    source_right(src_full, xs, 0, rows_here)
    await_recv(tgt_blocks.at[0], TGT_C)
    for k in range(n_chip):
        away = lax.rem(k % 4 - depth + 4, 4)
        at = away + (away // 2) * (5 - 2 * away)
        tgt_full[8 * k : 8 * k + 8, :] = jnp.concatenate([tgt_blocks[0, k // 4, at], tgt_blocks[1, k // 4, at]], axis=0)
    feature_major(tgt_full, ys)

    mixed = lax.dot_general(
        weights[...], ys[256:512, :], (((1,), (1,)), ((), ())), preferred_element_type=F32
    )
    terms[:, 0:256], terms[:, 256:512] = split(mixed)
    part = jnp.dot(xs[...], terms[...], preferred_element_type=F32)
    part = part[:, 0:256] + part[:, 256:512]
    at8 = lax.broadcasted_iota(jnp.int32, (8, 128), 0)
    lane8 = lax.broadcasted_iota(jnp.int32, (8, 128), 1)
    edge = jnp.where(at8 < 2, part[128:136, 0:128], 0.0)
    corner = part[128:136, 128:256]
    corner = jnp.concatenate([corner[6:8], corner[0:6]], axis=0)
    edge = jnp.where((at8 >= 2) & (at8 < 4), corner, edge)
    side = jnp.where(at8 < 2, part[0:128, 128:256].T[0:8], 0.0)
    for s in range(group):
        parts[s, 0:8, :] = part[8 * s : 8 * s + 8, 0:128]
        one = edge[s : s + 1] if s < 8 else side[s - 8 : s - 7]
        parts[s, 8:16, :] = jnp.where(at8 == 0, one, 0.0)

    def slot_of(peer):
        return lax.rem(peer[0], 2) * n_col + peer[1]

    for peer in group_peers:
        put(parts.at[slot_of(peer)], gathered.at[slot], SCATTER, peer)
    gathered[slot] = parts[slot]
    state_major(src_full, xt)
    await_recv(gathered.at[0 : group - 1], SCATTER)
    total = gathered[0]
    for k in range(1, group):
        total = total + gathered[k]
    middle[chip] = total
    for peer in chip_peers:
        put(middle.at[chip], middle.at[chip], MIDDLE, peer)
    pot_tgt[...] = prior_ref[...] * (LOG2E / EPSILON)
    await_recv(middle.at[0 : n_chip - 1], MIDDLE)
    total = middle[0]
    for k in range(1, n_chip):
        total = total + middle[k]
    core[slot] = total
    for peer in group_peers:
        put(core.at[slot], core.at[slot], SPREAD, peer)
    await_recv(core.at[0 : group - 1], SPREAD)

    scale = -2.0 * LOG2E / (EPSILON * total_src * total_tgt)
    main = jnp.concatenate([core[s, 0:8, :] for s in range(group)], axis=0) * (4.0 * scale)
    src_q, src_one = core[0, 8:9, :], core[1, 8:9, :]
    corner_q, corner_one = core[2, 8:9, :], core[3, 8:9, :]
    tgt_q, tgt_one = core[8, 8:9, :], core[9, 8:9, :]

    def pattern(at, first, second):
        value = jnp.where((at == 0) | (at == 2) | (at == 4), first, 0.0)
        return jnp.where((at == 1) | (at == 5), second, value)

    at16 = lax.broadcasted_iota(jnp.int32, (128, 128), 0)
    lane16 = lax.broadcasted_iota(jnp.int32, (128, 128), 1)
    lower_left = pattern(at16, src_one, src_q) * (-2.0 * scale)
    upper_right = pattern(at16, tgt_one, tgt_q).T * (-2.0 * scale)
    lower_right = pattern(
        at16,
        pattern(lane16, corner_one[:, 1:2], corner_one[:, 0:1]),
        pattern(lane16, corner_q[:, 1:2], corner_q[:, 0:1]),
    ) * scale
    left = jnp.concatenate([main, lower_left], axis=0)
    right = jnp.concatenate([upper_right, lower_right], axis=0)
    left_high, left_low = split(left)
    right_high, right_low = split(right)
    right_lane = lax.broadcasted_iota(jnp.int32, (256, 128), 1)
    ext = jnp.where(right_lane < 4, right_high.astype(F32), right_low.astype(F32)).astype(BF16)
    factor = jnp.concatenate([left_high, left_high, left_low, ext], axis=1)

    def factor_strip(n):
        cols = pl.ds(pl.multiple_of(n * 256, 256), 256)
        u = jnp.dot(factor, ys[:, cols], preferred_element_type=F32)
        high, low = split(u[0:128])
        us[0:128, cols] = high
        us[128:256, cols] = high
        us[256:384, cols] = low
        high, low = split(u[128:256])
        at = lax.broadcasted_iota(jnp.int32, (128, 256), 0)
        us[384:512, cols] = jnp.where(at < 4, high.astype(F32), low.astype(F32)).astype(BF16)

    n_strips = cols_here // 256

    def cost_of(n):
        lanes = pl.ds(pl.multiple_of(n * 512, 512), 512)
        cost[:, lanes] = jnp.dot(xt[...], us[:, lanes], preferred_element_type=F32)

    def cost_strip(n, carry):
        cost_of(n)
        factor_strip(2 * n + 2)
        factor_strip(2 * n + 3)
        return carry

    factor_strip(0)
    factor_strip(1)
    lax.fori_loop(0, n_strips // 2 - 1, cost_strip, 0)
    cost_of(n_strips // 2 - 1)

    n_part = half // 128
    n_lanes = cols_here // 2
    for sweep in range(SWEEPS):
        for h in range(2):
            mine_now = by_col.at[sweep, h, col]

            def block(b, carry):
                for q in range(8):
                    row_partial(h * half + b * 64 + 8 * q, pot_tgt, cost, row_tops, row_sums)
                return carry

            lax.fori_loop(0, half // 64, block, 0)
            for b in range(n_part):
                mine_now[b : b + 1, :] = row_finish(h * half + 128 * b, row_tops, row_sums)
            for peer in col_peers:
                put(mine_now, mine_now, ROWS + 2 * sweep + h, peer)
        f = []
        for h in range(2):
            await_recv(by_col.at[sweep, h, 0 : n_col - 1], ROWS + 2 * sweep + h)
            f.append(-math.log2(total_src) - combine(by_col.at[sweep, h]))
            down_rows(f[h], pot, h * half)

            for j in range(2):
                out = by_pair.at[sweep, j, core_id] if h else None

                def strip(n, carry):
                    col_strip(n, j * n_lanes, h * half, half, pot, cost, tops, sums, out)
                    return carry

                lax.fori_loop(0, n_lanes // STRIP, strip, 0)
                if h:
                    put(out, out, PAIR + 2 * sweep + j, pair_peer)
        for j in range(2):
            await_recv(by_pair.at[sweep, j, 0], PAIR + 2 * sweep + j)
            mine_now = by_chip.at[sweep, j, chip]
            mine_now[...] = combine(by_pair.at[sweep, j])
            for peer in chip_peers:
                put(mine_now, mine_now, CHIPS + 2 * sweep + j, peer)
        g = []
        for j in range(2):
            await_recv(by_chip.at[sweep, j, 0 : n_chip - 1], CHIPS + 2 * sweep + j)
            g.append(-math.log2(total_tgt) - combine(by_chip.at[sweep, j]))
        pot_tgt[...] = jnp.concatenate(g, axis=0)
    f_ref[...] = jnp.concatenate(f, axis=0) * (EPSILON / LOG2E)
    g_ref[...] = jnp.concatenate(g, axis=0) * (EPSILON / LOG2E)

    for h in range(2):
        await_send(block_at(col, h), SRC_Z + h)
        for k in range(2):
            await_send(block_at(col, h), FAR + 2 * k + h)
            for d in range(2):
                await_send(block_at(col, h), NEAR + 4 * d + 2 * k + h)
    await_send(tgt_blocks.at[0, 0, 0:2], TGT_Z)
    await_send(tgt_blocks.at[0, 0, 0], TGT_Z2)
    await_send(tgt_blocks.at[0, 0 : n_y - 1, 0:3], TGT_Y)
    await_send(tgt_blocks.at[0, 0 : n_y - 1, 3], TGT_Y2)
    await_send(tgt_blocks.at[0], TGT_C)
    await_send(gathered.at[0 : group - 1], SCATTER)
    await_send(middle.at[0 : n_chip - 1], MIDDLE)
    await_send(core.at[0 : group - 1], SPREAD)
    for sweep in range(SWEEPS):
        for h in range(2):
            await_send(by_col.at[sweep, h, 0 : n_col - 1], ROWS + 2 * sweep + h)
        for j in range(2):
            await_send(by_pair.at[sweep, j, 0], PAIR + 2 * sweep + j)
            await_send(by_chip.at[sweep, j, 0 : n_chip - 1], CHIPS + 2 * sweep + j)


def solution(mesh):
    n_row, n_col = mesh.shape["row"], mesh.shape["col"]
    n_chip = n_row // 2
    group = 2 * n_col

    def local(src_pos, tgt_pos, coupling, prior_tgt):
        rows, cols = coupling.shape
        vmem = pl.BlockSpec(memory_space=pltpu.VMEM)
        anywhere = pl.BlockSpec(memory_space=pl.ANY)
        f, g = pl.pallas_call(
            lambda *refs: kernel(n_row, n_col, *refs),
            out_shape=[
                jax.ShapeDtypeStruct((rows // 128, 128), F32),
                jax.ShapeDtypeStruct((cols // 128, 128), F32),
            ],
            in_specs=[anywhere, anywhere, anywhere, vmem],
            out_specs=[vmem, vmem],
            scratch_shapes=[
                pltpu.VMEM((rows, cols), BF16),
                pltpu.VMEM((128, rows), F32),
                pltpu.VMEM((2, n_chip // 4, 4, 4, cols), F32),
                pltpu.VMEM((128, cols), F32),
                pltpu.VMEM((144, rows), BF16),
                pltpu.VMEM((rows, 512), BF16),
                pltpu.VMEM((512, cols), BF16),
                pltpu.VMEM((512, cols), BF16),
                pltpu.VMEM((rows, 512), BF16),
                pltpu.VMEM((group, 16, 128), F32),
                pltpu.VMEM((group, 16, 128), F32),
                pltpu.VMEM((n_chip, 16, 128), F32),
                pltpu.VMEM((group, 16, 128), F32),
                pltpu.VMEM((rows, cols), F32),
                pltpu.VMEM((rows, 128), F32),
                pltpu.VMEM((cols // 128, 128), F32),
                pltpu.VMEM((8, cols), F32),
                pltpu.VMEM((8, cols), F32),
                pltpu.VMEM((rows, 128), F32),
                pltpu.VMEM((rows, 128), F32),
                pltpu.VMEM((SWEEPS, 2, n_col, rows // 256, 128), F32),
                pltpu.VMEM((SWEEPS, 2, 2, cols // 256, 128), F32),
                pltpu.VMEM((SWEEPS, 2, n_chip, cols // 256, 128), F32),
                pltpu.SemaphoreType.DMA((SLOTS,)),
                pltpu.SemaphoreType.DMA((SLOTS,)),
            ],
            compiler_params=pltpu.CompilerParams(
                collective_id=0, has_side_effects=True, vmem_limit_bytes=63 * 2**20
            ),
        )(src_pos, tgt_pos, coupling, prior_tgt.reshape(cols // 128, 128))
        return f.reshape(rows), g.reshape(cols)

    placed = (P("col", "row"), P("row", "col"), P("row", "col"), P("col"))
    return jax.shard_map(
        local, mesh=mesh, in_specs=placed, out_specs=(P("row"), P("col")), check_vma=False
    )
```
